256 devices in a mesh: learn: 16 (over x, z_hi), tp: 4 (over y), dp: 4 (over z_lo, core).
Axes of the slice: x: 4, y: 4, z: 8 (z_hi: 4, z_lo: 2; z = z_hi * 2 + z_lo), core: 2. Of those that a mesh axis runs over, the one named last changes fastest.
Arguments:
- features: bfloat16 [32768, 8192], P(('learn', 'dp'), 'tp'), may hold values from -16 to 16
- kv_cotangent: bfloat16 [32768, 2048], P(('learn', 'dp'), 'tp'), may hold values from -0.032958984 to 0.032958984
- master_weight: float32 [8192, 2048], P(('learn', 'dp'), 'tp'), may hold values from -0.0625 to 0.0625
- first_moment: float32 [8192, 2048], P(('learn', 'dp'), 'tp'), may hold values from -1.2 to 1.2
- second_moment: float32 [8192, 2048], P(('learn', 'dp'), 'tp'), may hold values from 0.0001 to 0.01
- decode_inputs: bfloat16 [4, 128, 8192], P(None, ('learn', 'dp')), may hold values from -6 to 6
- queries: bfloat16 [4, 128, 8192], P(None, ('learn', 'dp'), 'tp'), may hold values from -120 to 120
- kv_cache: bfloat16 [2, 128, 8, 4096, 128], P(None, ('learn', 'dp'), 'tp'), may hold values from -6 to 6, as said below
- cache_lengths: int32 [128], P(('learn', 'dp')), may hold values from 1 to 4096, 264192 in all
Outputs:
- master_out: float32 [8192, 2048], P(('learn', 'dp'), 'tp')
- first_out: float32 [8192, 2048], P(('learn', 'dp'), 'tp')
- second_out: float32 [8192, 2048], P(('learn', 'dp'), 'tp')
- new_kv: bfloat16 [4, 128, 2048], P(None, ('learn', 'dp'), 'tp')
- attended: bfloat16 [4, 128, 8192], P(None, ('learn', 'dp'), 'tp')
The draws below stay inside these ranges and needn't reach their ends.
Inputs may be any that keep to these rules, and one draw needn't show every extreme that they name: `kv_cache`: normal entries; in some draws a cached key at position 1 is close to the key at position 0. `cache_lengths`: some row has exactly 4096 cached tokens.
All inputs are finite; a program needn't handle non-finite values. No bound on the sum of `cache_lengths` on one device may be relied on, other than what follows from the above.
Results may differ from the reference program's by a relative error of at most 0.005.
Values may be sent and summed in bfloat16 or wider, within the bound.
A program may use at most 128 MiB of HBM per device.

```python
import math
import jax
import jax.numpy as jnp
import numpy as np
from jax import lax

D = 8192
HQ = 64
KVH = 8
HD = 128
CTX = 4096
STEPS = 4
KVC = 2048
TOKENS = 32768
ROWS_ALL = 128


def cache_normal(key):
    values = jax.random.normal(key, (2, ROWS_ALL, KVH, CTX, HD), jnp.float32)
    return jnp.clip(values, -5.5, 5.5)


def draw_kv_cache(key, part):
    base_values = cache_normal(key)
    return base_values.astype(jnp.bfloat16)


def draw_queries(key, part):
    key = jax.random.fold_in(key, 13)
    noise = jax.random.normal(key, (STEPS, ROWS_ALL, KVH, HQ // KVH, HD), jnp.float32)
    values = noise
    values = jnp.clip(values, -120.0, 120.0)
    return values.reshape(STEPS, ROWS_ALL, HQ * HD).astype(jnp.bfloat16)


def raised(entries, rng, source, target, blocks, factor):
    def block_of(axis_at):
        return (jnp.arange(entries.shape[axis_at]) // (entries.shape[axis_at] // blocks)).reshape((-1,) + (1,) * (entries.ndim - 1 - axis_at))

    near = jax.random.permutation(rng, blocks)[block_of(target)]
    far = (block_of(target) + blocks // 2) % blocks
    return jnp.where((block_of(source) == near) | (block_of(source) == far), factor * entries, entries)


def steps_of(stream_key, shape, cuts, smallest, high):
    gain, own = 1.0, jax.random.fold_in(stream_key, 6)
    for position, shards_of in cuts:
        heights = jnp.exp(jax.random.uniform(jax.random.fold_in(own, position), (shards_of,), jnp.float32, smallest / len(cuts), high / len(cuts)))
        gain = gain * jnp.repeat(heights, shape[position] // shards_of).reshape([-1 if axis == position else 1 for axis in range(len(shape))])
    return gain


def split_up(count, total, reach, lean):
    weights = [(1 << 20) // math.isqrt(rank ** lean) + 1 for rank in range(2, count + 1)]
    surplus, given = total - reach - (count - 1), [1] * (count - 1)
    while surplus > 0:
        candidates = [i for i in range(count - 1) if given[i] < reach]
        pool, left = sum([weights[i] for i in candidates]), surplus
        for i in candidates:
            addition = min(reach - given[i], max(1, left * weights[i] // pool), surplus)
            given[i] = given[i] + addition
            surplus = surplus - addition
    return np.array([reach] + given)


def uneven_parts(own_key, number_of, total, most, skew):
    if number_of == 2:
        one = jax.random.randint(own_key, (), max(1, total - most), min(most, total - 1) + 1)
        return jnp.stack([one, total - one])
    tallies = jnp.asarray(split_up(number_of, total, most, skew), jnp.int32)
    couples = (number_of - 1) // 2
    donor, receiver = tallies[1:1 + 2 * couples:2], tallies[2:2 + 2 * couples:2]
    margin = jnp.minimum(donor - 1, most - receiver)
    moved = jax.random.randint(jax.random.fold_in(own_key, 1), (couples,), 0, 1 << 20) % (margin + 1)
    tallies = tallies.at[1:1 + 2 * couples:2].set(donor - moved).at[2:2 + 2 * couples:2].set(receiver + moved)
    return tallies[jax.random.permutation(jax.random.fold_in(own_key, 2), number_of)]


def centred(key, shape, scale, reach, cuts=(), held_as=jnp.bfloat16):
    values = jax.random.normal(key, shape, jnp.float32) * scale
    if len(cuts) > 0:
        values = steps_of(key, shape, cuts, -0.22, 0.18) * values
    return jnp.clip(values, min=-reach, max=reach).astype(held_as)


def bell_draw_with(stream_key, dims, scale, bound, shards, heavy, kind=jnp.bfloat16):
    values = scale * jax.random.normal(stream_key, dims, jnp.float32)
    if shards:
        values = values * steps_of(stream_key, dims, shards, -0.22, 0.18)
    return jnp.clip(raised(values, jax.random.fold_in(stream_key, 3), *heavy), -bound, bound).astype(kind)


def setup_inputs(seed: int = 0) -> dict:
    arg_keys = jax.random.split(jax.random.key(seed), 10)
    return {
        "features": bell_draw_with(arg_keys[0], (TOKENS, D), 1.0, 16.0, ((0, 64), (1, 4)), (0, 1, 64, 4.0)),
        "kv_cotangent": centred(arg_keys[1], (TOKENS, KVC), (1.0 / TOKENS ** 0.5), 0.032958984, ((0, 64), (1, 4))),
        "master_weight": centred(arg_keys[2], (D, KVC), D ** -0.5, 0.0625, ((0, 64), (1, 4)), jnp.float32),
        "first_moment": centred(arg_keys[3], (D, KVC), 0.2, 1.2, ((0, 64), (1, 4)), jnp.float32),
        "second_moment": jnp.clip(jnp.exp(math.log(0.01) - 4.6051702 * jax.random.uniform(arg_keys[4], (D, KVC), jnp.float32) ** steps_of(arg_keys[4], (D, KVC), ((0, 64), (1, 4)), -0.2, 0.2)), 0.0001, 0.01),
        "decode_inputs": centred(arg_keys[5], (STEPS, ROWS_ALL, D), 1.0, 6.0, ((1, 64),)),
        "queries": draw_queries(jax.random.fold_in(arg_keys[9], 71), 0),
        "kv_cache": draw_kv_cache(jax.random.fold_in(arg_keys[9], 71), 0),
        "cache_lengths": uneven_parts(arg_keys[8], ROWS_ALL, ROWS_ALL * CTX // 2 + CTX // 2, CTX, 1).astype(jnp.int32),
    }


learn_rate = 0.005
decay_rate = 0.1
first_fix = 1.0 - 0.9 ** 10
second_fix = 1.0 - 0.999 ** 10

def attend(queries, kv_cache, cache_lengths, new_kv):
    step_count, row_count = (queries.shape[0], queries.shape[1])
    heads_kv, slot_count, head_size = (kv_cache.shape[2], kv_cache.shape[3], kv_cache.shape[4])
    query_heads = queries.reshape(step_count, row_count, heads_kv, -1, head_size).astype(jnp.float32)
    recent = new_kv.reshape(step_count, row_count, heads_kv, 2, head_size).astype(jnp.float32)
    cache_keys = kv_cache[0].astype(jnp.float32)
    cache_values = kv_cache[1].astype(jnp.float32)
    score_scale = head_size ** (-0.5)
    cached = jnp.einsum('srhgd,rhpd->srhgp', query_heads, cache_keys) * score_scale
    positions = jnp.arange(slot_count, dtype=jnp.int32)
    allowed = positions[None, :] < cache_lengths[:, None]
    cached = jnp.where(allowed[None, :, None, None, :], cached, -jnp.inf)
    fresh = jnp.einsum('srhgd,jrhd->srhgj', query_heads, recent[:, :, :, 0, :]) * score_scale
    order = jnp.arange(step_count, dtype=jnp.int32)
    causal = order[None, :] <= order[:, None]
    fresh = jnp.where(causal[:, None, None, None, :], fresh, -jnp.inf)
    highest = jnp.maximum(lax.optimization_barrier(jnp.max(cached, axis=-1)), lax.optimization_barrier(jnp.max(fresh, axis=-1)))[..., None]
    cached_exp = jnp.exp(cached - highest)
    fresh_exp = jnp.exp(fresh - highest)
    denominator = lax.optimization_barrier(jnp.sum(cached_exp, axis=-1, keepdims=True)) + lax.optimization_barrier(jnp.sum(fresh_exp, axis=-1, keepdims=True))
    cached_weight = (cached_exp / denominator).astype(jnp.bfloat16).astype(jnp.float32)
    fresh_weight = (fresh_exp / denominator).astype(jnp.bfloat16).astype(jnp.float32)
    result = jnp.einsum('srhgp,rhpd->srhgd', cached_weight, cache_values)
    result = result + jnp.einsum('srhgj,jrhd->srhgd', fresh_weight, recent[:, :, :, 1, :])
    return result.reshape(step_count, row_count, -1).astype(jnp.bfloat16)

def reference(features, kv_cotangent, master_weight, first_moment, second_moment, decode_inputs, queries, kv_cache, cache_lengths):
    gradient = lax.dot_general(features, kv_cotangent, (((0,), (0,)), ((), ())), preferred_element_type=jnp.float32)
    first_out = 0.9 * first_moment + 0.1 * gradient
    second_out = 0.999 * second_moment + 0.001 * gradient * gradient
    update = first_out / first_fix / (jnp.sqrt(second_out / second_fix) + 1e-08)
    master_out = master_weight - learn_rate * (update + decay_rate * master_weight)
    rollout_weight = master_out.astype(jnp.bfloat16)
    step_count, row_count, width = decode_inputs.shape
    flat_inputs = decode_inputs.reshape(step_count * row_count, width)
    new_kv = jnp.dot(flat_inputs, rollout_weight, preferred_element_type=jnp.float32).astype(jnp.bfloat16)
    new_kv = new_kv.reshape(step_count, row_count, -1)
    attended = attend(queries, kv_cache, cache_lengths, new_kv)
    return (master_out, first_out, second_out, new_kv, attended)
```

```python
import jax
import jax.numpy as jnp
from jax import lax
from jax.sharding import PartitionSpec as P

learn_rate = 0.005
decay_rate = 0.1
first_fix = 1.0 - 0.9**10
second_fix = 1.0 - 0.999**10


def attend(queries, kv_cache, cache_lengths, new_kv):
    step_count, row_count = (queries.shape[0], queries.shape[1])
    heads_kv, slot_count, head_size = (kv_cache.shape[2], kv_cache.shape[3], kv_cache.shape[4])
    query_heads = queries.reshape(step_count, row_count, heads_kv, -1, head_size)
    recent = new_kv.reshape(step_count, row_count, heads_kv, 2, head_size)
    score_scale = head_size ** (-0.5)
    cached = (
        jnp.einsum(
            "srhgd,rhpd->srhgp", query_heads, kv_cache[0], preferred_element_type=jnp.float32
        )
        * score_scale
    )
    positions = jnp.arange(slot_count, dtype=jnp.int32)
    allowed = positions[None, :] < cache_lengths[:, None]
    cached = jnp.where(allowed[None, :, None, None, :], cached, -jnp.inf)
    fresh = (
        jnp.einsum(
            "srhgd,jrhd->srhgj",
            query_heads,
            recent[:, :, :, 0, :],
            preferred_element_type=jnp.float32,
        )
        * score_scale
    )
    order = jnp.arange(step_count, dtype=jnp.int32)
    causal = order[None, :] <= order[:, None]
    fresh = jnp.where(causal[:, None, None, None, :], fresh, -jnp.inf)
    highest = jnp.maximum(jnp.max(cached, axis=-1), jnp.max(fresh, axis=-1))[..., None]
    cached_exp = jnp.exp(cached - highest)
    fresh_exp = jnp.exp(fresh - highest)
    denominator = jnp.sum(cached_exp, axis=-1, keepdims=True) + jnp.sum(
        fresh_exp, axis=-1, keepdims=True
    )
    cached_weight = (cached_exp / denominator).astype(jnp.bfloat16)
    fresh_weight = (fresh_exp / denominator).astype(jnp.bfloat16)
    result = jnp.einsum(
        "srhgp,rhpd->srhgd", cached_weight, kv_cache[1], preferred_element_type=jnp.float32
    )
    result = result + jnp.einsum(
        "srhgj,jrhd->srhgd", fresh_weight, recent[:, :, :, 1, :], preferred_element_type=jnp.float32
    )
    return result.reshape(step_count, row_count, -1).astype(jnp.bfloat16)


def shards(
    features,
    kv_cotangent,
    master_weight,
    first_moment,
    second_moment,
    decode_inputs,
    queries,
    kv_cache,
    cache_lengths,
):
    token_count, own_columns = kv_cotangent.shape
    tp_size = lax.axis_size("tp")
    dp_size = lax.axis_size("dp")
    learn_size = lax.axis_size("learn")
    high = learn_size // tp_size
    cotangents = lax.all_gather(kv_cotangent, "tp", axis=0)
    part = own_columns // tp_size
    cotangents = cotangents.reshape(tp_size, token_count, tp_size, part)
    products = jnp.einsum(
        "tr,ctsk->srck", features, cotangents, preferred_element_type=jnp.float32
    )
    products = products.reshape(-1, tp_size * part)
    summed = lax.psum_scatter(products, ("learn", "dp"), scatter_dimension=0, tiled=True)
    summed = summed.reshape(-1, tp_size, part)
    summed = lax.all_to_all(summed, "tp", 1, 0, tiled=False)
    groups = [[one * high + low for one in range(tp_size)] for low in range(high)]
    summed = lax.all_to_all(summed, "learn", 0, 1, axis_index_groups=groups, tiled=False)
    gradient = summed.reshape(-1, own_columns)
    first_out = 0.9 * first_moment + 0.1 * gradient
    second_out = 0.999 * second_moment + 0.001 * gradient * gradient
    update = first_out / first_fix / (jnp.sqrt(second_out / second_fix) + 1e-08)
    master_out = master_weight - learn_rate * (update + decay_rate * master_weight)
    rollout_weight = master_out.astype(jnp.bfloat16)
    steps, rows, width = decode_inputs.shape
    devices = learn_size * dp_size
    spread = decode_inputs.reshape(steps, rows, devices, width // devices)
    spread = lax.all_to_all(spread, ("learn", "dp"), 2, 0, tiled=False)
    partial = jnp.einsum("nk,kc->nc", spread.reshape(-1, width // devices), rollout_weight, preferred_element_type=jnp.float32)
    projected = lax.psum_scatter(partial, ("learn", "dp"), scatter_dimension=0, tiled=True)
    projected = projected.reshape(steps, rows, own_columns)
    new_kv = projected.astype(jnp.bfloat16)
    attended = attend(queries, kv_cache, cache_lengths, new_kv)
    return (master_out, first_out, second_out, new_kv, attended)


def solution(mesh):
    in_specs = (
        P(("learn", "dp"), "tp"),
        P(("learn", "dp"), "tp"),
        P(("learn", "dp"), "tp"),
        P(("learn", "dp"), "tp"),
        P(("learn", "dp"), "tp"),
        P(None, ("learn", "dp"), None),
        P(None, ("learn", "dp"), "tp"),
        P(None, ("learn", "dp"), "tp", None, None),
        P(("learn", "dp")),
    )
    out_specs = (
        P(("learn", "dp"), "tp"),
        P(("learn", "dp"), "tp"),
        P(("learn", "dp"), "tp"),
        P(None, ("learn", "dp"), "tp"),
        P(None, ("learn", "dp"), "tp"),
    )
    return jax.shard_map(shards, mesh=mesh, in_specs=in_specs, out_specs=out_specs, check_vma=False)
```

```python
import functools
import types

import jax
import jax.numpy as jnp
from jax import lax
from jax.experimental import pallas as pl
from jax.experimental.pallas import tpu as pltpu
from jax.sharding import PartitionSpec as P

learn_rate = 0.005
decay_rate = 0.1
first_fix = 1.0 - 0.9**10
second_fix = 1.0 - 0.999**10

MESH = pl.DeviceIdType.MESH
UNITS = 8
NX, NY, NZ = 4, 4, 8
LAGS = (1, 4, 7, 10)

bf16 = jnp.bfloat16
f32 = jnp.float32


def position():
    learn, dp = lax.axis_index("learn"), lax.axis_index("dp")
    return learn // 4, lax.axis_index("tp"), (learn % 4) * 2 + dp // 2, dp % 2


def device(x, y, z, core):
    return {"learn": x * 4 + z // 2, "tp": y, "dp": (z % 2) * 2 + core}


def send(source, target, send_sem, recv_sem, where):
    return pltpu.make_async_remote_copy(
        src_ref=source,
        dst_ref=target,
        send_sem=send_sem,
        recv_sem=recv_sem,
        device_id=where,
        device_id_type=MESH,
    )


def unit_place(unit):
    pair, odd = unit // 2, unit % 2
    middle = ((pair + 1) // 2) % 2
    return middle * (1 + 2 * odd) + 2 * (pair // 3), (1 - middle) * odd + middle * (pair // 2)


def adam(gradient, master, first, second):
    first = 0.9 * first + 0.1 * gradient
    second = 0.999 * second + 0.001 * gradient * gradient
    update = (first / first_fix) / (jnp.sqrt(second / second_fix) + 1e-08)
    return master - learn_rate * (update + decay_rate * master), first, second


def scratch(rows, columns, tokens, slots, head):
    part, half = rows // 4, columns // 2
    dma = pltpu.SemaphoreType.DMA
    return dict(
        feat=pltpu.VMEM((tokens, 16 * rows), bf16),
        turned=pltpu.VMEM((2, NZ, rows, tokens), bf16),
        cot=pltpu.VMEM((UNITS, tokens, half), bf16),
        core_send=pltpu.VMEM((UNITS, NZ, 4, part, half), bf16),
        core_recv=pltpu.VMEM((UNITS, NZ, 4, part, half), bf16),
        mine=pltpu.VMEM((NZ, 4, part, half), f32),
        keep=pltpu.VMEM((UNITS, 2, 2, 4, part, half), f32),
        x1_send=pltpu.VMEM((UNITS, 2, 2, 4, part, half), bf16),
        x1_recv=pltpu.VMEM((UNITS, 2, 2, 4, part, half), bf16),
        x2_send=pltpu.VMEM((UNITS, 2, 4, part, half), bf16),
        x2_recv=pltpu.VMEM((UNITS, 2, 4, part, half), bf16),
        z_sum=pltpu.VMEM((NZ, part, half), f32),
        z_own=pltpu.VMEM((UNITS, part, half), f32),
        z_send=pltpu.VMEM((UNITS, NZ - 1, part, half), bf16),
        z_recv=pltpu.VMEM((UNITS, NZ - 1, part, half), bf16),
        t_send=pltpu.VMEM((UNITS, part, half), f32),
        grad=pltpu.VMEM((2, 4, part, half), f32),
        kv=pltpu.VMEM((2, 2, 2, slots, head), bf16),
        state=pltpu.VMEM((3, rows, columns), f32),
        rollout=pltpu.VMEM((rows, columns), bf16),
        x_mine=pltpu.VMEM((8, 64 * rows), f32),
        x_pair=pltpu.VMEM((8, 64 * rows), f32),
        xz_send=pltpu.VMEM((NZ - 1, NX, 16, rows), bf16),
        xz_recv=pltpu.VMEM((NZ - 1, NX, 16, rows), bf16),
        xx_send=pltpu.VMEM((NX - 1, NZ, 16, rows), bf16),
        xx_recv=pltpu.VMEM((NX - 1, NZ, 16, rows), bf16),
        xx_own=pltpu.VMEM((NX, 16, rows), bf16),
        x_own=pltpu.VMEM((NZ, 16, rows), bf16),
        y_part=pltpu.VMEM((NX, NZ, 2, 8, columns), f32),
        y_core=pltpu.VMEM((NX, NZ, 8, columns), f32),
        yx_send=pltpu.VMEM((NX - 1, NZ, 8, columns), f32),
        yx_recv=pltpu.VMEM((NX - 1, NZ, 8, columns), f32),
        y_sum=pltpu.VMEM((NZ, 8, columns), f32),
        yz_recv=pltpu.VMEM((NZ - 1, 8, columns), f32),
        scores=pltpu.VMEM((32, slots), f32),
        query=pltpu.VMEM((2, 8, 8, head), f32),
        answer=pltpu.VMEM((2, 8, 8, head), f32),
        att=pltpu.VMEM((2, 64, head), f32),
        top=pltpu.VMEM((2, 64, head), f32),
        total=pltpu.VMEM((2, 64, head), f32),
        load_sem=dma((7,)),
        out_sem=dma((2, 4)),
        cot_ss=dma((6,)),
        cot_rs=dma((UNITS,)),
        core_ss=dma((UNITS,)),
        core_rs=dma((UNITS,)),
        x1_ss=dma((UNITS, 2)),
        x1_rs=dma((UNITS, 2)),
        x2_ss=dma((UNITS, 2)),
        x2_rs=dma((UNITS, 2)),
        z_ss=dma((UNITS,)),
        z_rs=dma((UNITS,)),
        t_ss=dma((UNITS,)),
        t_rs=dma((2, 4)),
        xc_sem=dma((2,)),
        xz_sem=dma((2,)),
        xx_ss=dma((3,)),
        xx_rs=dma((3,)),
        yc_ss=dma((4,)),
        yc_rs=dma((4,)),
        yx_ss=dma((3,)),
        yx_rs=dma((3,)),
        yz_sem=dma((2,)),
    )


def kernel(names, *refs):
    (lengths, q_ref, x_ref, f_hbm, c_hbm, w_hbm, m_hbm, v_hbm, kv_hbm) = refs[:9]
    (grad_out, new_out, att_out) = refs[9:12]
    r = types.SimpleNamespace(**dict(zip(names, refs[12:])))
    x, y, z, core = position()
    other = 1 - core
    flip, mirror = x + 1 - 2 * (x % 2), 3 - x
    first_partner, second_partner = (flip, mirror), (mirror, flip)
    rows, columns = r.rollout.shape
    part, half = rows // 4, columns // 2
    tokens = r.feat.shape[0]
    slots, head = r.kv.shape[3:]
    scale = head**-0.5

    loads = [
        pltpu.make_async_copy(source, target, r.load_sem.at[i])
        for i, (source, target) in enumerate(
            (
                (c_hbm.at[:, pl.ds(0, half)], r.cot.at[0]),
                (f_hbm, r.feat),
                (c_hbm.at[:, pl.ds(half, half)], r.cot.at[1]),
                (kv_hbm, r.kv),
                (w_hbm, r.state.at[0]),
                (m_hbm, r.state.at[1]),
                (v_hbm, r.state.at[2]),
            )
        )
    ]
    for load in loads[:3]:
        load.start()

    for s in range(4):
        r.x_mine[2 * s : 2 * s + 2] = x_ref[s].astype(f32)

    barrier = pltpu.get_barrier_semaphore()

    def greet(where):
        pl.semaphore_signal(barrier, inc=1, device_id=where, device_id_type=MESH)

    greet(device(x, y, z, other))
    for k in range(1, NX):
        greet(device((x + k) % NX, y, z, core))
    for k in range(1, NZ):
        greet(device(x, y, (z + k) % NZ, core))
    for k in (1, NY - 1):
        greet(device(x, (y + k) % NY, z, core))
    for k in range(4):

        @pl.when(jnp.logical_or(x != y, y != k))
        def _():
            greet(device(y, k, z, core))

        @pl.when(jnp.logical_or(x != y, x != k))
        def _():
            greet(device(k, x, z, core))

    same = (4 - (x - y + 4) % 4) // 4
    pl.semaphore_wait(barrier, 1 + (NX - 1) + (NZ - 1) + 2 + 8 - 2 * same)

    def cot_copy(index, source, target, step):
        return send(
            r.cot.at[source],
            r.cot.at[target],
            r.cot_ss.at[index],
            r.cot_rs.at[target],
            device(x, (y + step) % NY, z, core),
        )

    loads[0].wait()
    cot_copy(0, 0, 2, NY - 1).start()
    cot_copy(1, 0, 3, 1).start()
    x_swap = send(r.x_mine, r.x_pair, r.xc_sem.at[0], r.xc_sem.at[1], device(x, y, z, other))
    x_swap.start()
    loads[2].wait()
    cot_copy(2, 1, 4, NY - 1).start()
    cot_copy(3, 1, 5, 1).start()
    loads[1].wait()
    for load in loads[3:]:
        load.start()

    def turn(side):
        for row_block in range(NZ):
            columns_of = pl.ds(pl.multiple_of((row_block * 2 + side) * rows, rows), rows)
            r.turned[side, row_block] = r.feat[:, columns_of].T

    def multiply(side, unit, store):
        def step(i, carry):
            left = r.turned[side, pl.ds(2 * i, 2)].reshape(2 * rows, tokens)
            product = jnp.dot(left, r.cot[unit], preferred_element_type=f32)
            store(i, product.reshape(2, 4, part, half))
            return carry

        lax.fori_loop(0, NZ // 2, step, 0)

    def core_copy(unit):
        return send(
            r.core_send.at[unit],
            r.core_recv.at[unit],
            r.core_ss.at[unit],
            r.core_rs.at[unit],
            device(x, y, z, other),
        )

    def x1_copy(unit, side):
        return send(
            r.x1_send.at[unit, side],
            r.x1_recv.at[unit, side],
            r.x1_ss.at[unit, side],
            r.x1_rs.at[unit, side],
            device(first_partner[side], y, z, core),
        )

    def x2_copy(unit, side):
        return send(
            r.x2_send.at[unit, side],
            r.x2_recv.at[unit, side],
            r.x2_ss.at[unit, side],
            r.x2_rs.at[unit, side],
            device(second_partner[side], y, z, core),
        )

    def z_copy(unit, k):
        return send(
            r.z_send.at[unit, k - 1],
            r.z_recv.at[unit, k - 1],
            r.z_ss.at[unit],
            r.z_rs.at[unit],
            device(x, y, (z + k) % NZ, core),
        )

    def z_all(unit):
        return send(
            r.z_send.at[unit],
            r.z_recv.at[unit],
            r.z_ss.at[unit],
            r.z_rs.at[unit],
            device(x, y, (z + 1) % NZ, core),
        )

    def t_copy(unit):
        away, which = unit_place(unit)
        return send(
            r.t_send.at[unit],
            r.grad.at[which, x],
            r.t_ss.at[unit],
            r.t_rs.at[which, x],
            device(y, (y + away) % NY, z, core),
        )

    def stage0(unit):
        @pl.when(unit >= 2)
        def _():
            send(
                r.cot.at[unit],
                r.cot.at[unit],
                r.cot_ss.at[0],
                r.cot_rs.at[unit],
                device(x, (y + 1) % NY, z, core),
            ).wait_recv()

        @pl.when(unit == 3)
        def _():
            cot_copy(4, 3, 6, 1).start()

        @pl.when(unit == 4)
        def _():
            cot_copy(5, 4, 7, NY - 1).start()

        def store(i, product):
            r.core_send[unit, pl.ds(2 * i, 2)] = product.astype(bf16)

        multiply(other, unit, store)
        core_copy(unit).start()

    def stage1(unit):
        def store(i, product):
            r.mine[pl.ds(2 * i, 2)] = product

        multiply(core, unit, store)
        core_copy(unit).wait()
        for side in range(2):
            partner = first_partner[side]
            away = (partner, (3 - partner, partner + 1 - 2 * (partner % 2))[side])
            for k in range(2):
                for at in range(4):
                    row_block = side * 4 + at
                    r.x1_send[unit, side, k, at] = (
                        r.mine[row_block, away[k]]
                        + r.core_recv[unit, row_block, away[k]].astype(f32)
                    ).astype(bf16)
            x1_copy(unit, side).start()
        for side in range(2):
            near = (x, second_partner[side])
            for k in range(2):
                for at in range(4):
                    row_block = side * 4 + at
                    r.keep[unit, side, k, at] = r.mine[row_block, near[k]] + r.core_recv[
                        unit, row_block, near[k]
                    ].astype(f32)

    def stage2(unit):
        for side in range(2):
            x1_copy(unit, side).wait()
            r.x2_send[unit, side] = (
                r.keep[unit, side, 1] + r.x1_recv[unit, side, 1].astype(f32)
            ).astype(bf16)
            x2_copy(unit, side).start()
        for side in range(2):
            r.keep[unit, side, 0] += r.x1_recv[unit, side, 0].astype(f32)

    def stage3(unit):
        for side in range(2):
            x2_copy(unit, side).wait()
            for at in range(4):
                r.z_sum[side * 4 + at] = r.keep[unit, side, 0, at] + r.x2_recv[
                    unit, side, at
                ].astype(f32)
        for k in (4, 3, 5, 2, 6, 1, 7):
            r.z_send[unit, k - 1] = r.z_sum[(z + k) % NZ].astype(bf16)
            z_copy(unit, k).start()
        r.z_own[unit] = r.z_sum[z]

    def stage4(unit):
        z_all(unit).wait()
        total = r.z_own[unit]
        for k in range(NZ - 1):
            total = total + r.z_recv[unit, k].astype(f32)
        away, which = unit_place(unit)
        here = jnp.logical_and(x == y, away == 0)

        @pl.when(here)
        def _():
            r.grad[which, x] = total

        @pl.when(jnp.logical_not(here))
        def _():
            r.t_send[unit] = total
            t_copy(unit).start()

    def spread_z():
        x_swap.wait()
        for k in list(range(1, NZ)) + [0]:
            block = (z + k) % NZ
            for to in range(NX):
                at = pl.ds(pl.multiple_of((to * 16 + block * 2 + core) * rows, rows), rows)
                own, pair = r.x_mine[:, at], r.x_pair[:, at]
                low, high = jnp.where(core == 0, own, pair), jnp.where(core == 0, pair, own)
                value = jnp.concatenate([low, high], axis=0).astype(bf16)
                if k > 0:
                    r.xz_send[k - 1, to] = value
                else:
                    r.xx_own[to] = value
            if k > 0:
                send(
                    r.xz_send.at[k - 1],
                    r.xz_recv.at[k - 1],
                    r.xz_sem.at[0],
                    r.xz_sem.at[1],
                    device(x, y, block, core),
                ).start()

    def xx_copy(k):
        return send(
            r.xx_send.at[k - 1],
            r.xx_recv.at[k - 1],
            r.xx_ss.at[k - 1],
            r.xx_rs.at[k - 1],
            device((x + k) % NX, y, z, core),
        )

    def spread_x():
        send(
            r.xz_send,
            r.xz_recv,
            r.xz_sem.at[0],
            r.xz_sem.at[1],
            device(x, y, (z + 1) % NZ, core),
        ).wait()
        for k in range(NX):
            to = (x + k) % NX
            target = r.x_own if k == 0 else r.xx_send.at[k - 1]
            target[z] = r.xx_own[to]
            for j in range(1, NZ):
                target[(z + NZ - j) % NZ] = r.xz_recv[j - 1, to]
            if k > 0:
                xx_copy(k).start()

    chunk = min(1024, slots)

    def cached(pair):
        row, kv_head = pair // 2, pair % 2
        query = r.query[kv_head].reshape(4, 2, 8, head)
        query = jnp.where(row == 0, query[:, 0], query[:, 1]).reshape(32, head).astype(bf16)

        def score(i, highest):
            at = pl.ds(pl.multiple_of(i * chunk, chunk), chunk)
            value = lax.dot_general(
                query,
                r.kv[0, row, kv_head, at],
                (((1,), (1,)), ((), ())),
                preferred_element_type=f32,
            )
            places = i * chunk + lax.broadcasted_iota(jnp.int32, value.shape, 1)
            value = jnp.where(places < lengths[row], value * scale, -jnp.inf)
            r.scores[:, at] = value
            return jnp.maximum(highest, jnp.max(value, axis=1, keepdims=True))

        highest = lax.fori_loop(0, slots // chunk, score, jnp.full((32, 1), -jnp.inf, f32))

        def weigh(i, carry):
            total, result = carry
            at = pl.ds(pl.multiple_of(i * chunk, chunk), chunk)
            weight = jnp.exp(r.scores[:, at] - highest)
            total = total + jnp.sum(weight, axis=1, keepdims=True)
            result = result + jnp.dot(
                weight.astype(bf16), r.kv[1, row, kv_head, at], preferred_element_type=f32
            )
            return total, result

        total, result = lax.fori_loop(
            0, slots // chunk, weigh, (jnp.zeros((32, 1), f32), jnp.zeros((32, head), f32))
        )
        highest = jnp.broadcast_to(highest, (32, head))
        total = jnp.broadcast_to(total, (32, head))
        for s in range(4):
            at = pl.ds(pl.multiple_of(s * 16 + row * 8, 8), 8)
            one = slice(s * 8, s * 8 + 8)
            r.att[kv_head, at] = result[one]
            r.top[kv_head, at] = highest[one]
            r.total[kv_head, at] = total[one]

    turn(other)

    def during(t, lag, stage):
        @pl.when(jnp.logical_and(t >= lag, t < UNITS + lag))
        def _():
            stage(t - lag)

    def tick(t, carry):
        during(t, LAGS[3], stage4)
        during(t, LAGS[2], stage3)
        during(t, LAGS[1], stage2)
        during(t, LAGS[0], stage1)
        during(t, 0, stage0)

        @pl.when(t == 0)
        def _():
            turn(core)
            spread_z()

        @pl.when(t == 2)
        def _():
            spread_x()
            loads[3].wait()
            asked = jnp.concatenate([q_ref[s].astype(f32) for s in range(4)], axis=0)
            for h in range(2):
                for g in range(8):
                    r.query[h, :, g, :] = asked[:, (h * 8 + g) * head : (h * 8 + g + 1) * head]

        during(t, 3, lambda pair: pl.when(pair < 4)(lambda: cached(pair)))

        @pl.when(t == UNITS)
        def _():
            for k in range(1, NX):
                xx_copy(k).wait()
            for k in range(4, 7):
                loads[k].wait()
            for index in range(6):
                cot_copy(index, index % 2, 2 + index, 1).wait_send()

        return carry

    lax.fori_loop(0, UNITS + LAGS[3], tick, 0)

    stores = []
    for s in range(4):
        for which in range(2):

            @pl.when(jnp.logical_or(x != y, x != s))
            def _():
                send(
                    r.t_send.at[0],
                    r.grad.at[which, s],
                    r.t_ss.at[0],
                    r.t_rs.at[which, s],
                    device(x, (y + 1) % NY, z, core),
                ).wait_recv()

            at = (pl.ds(s * part, part), pl.ds(which * half, half))
            gradient = r.grad[which, s]
            master, _, _ = adam(
                gradient, *(r.state[i, at[0], at[1]] for i in range(3))
            )
            r.rollout[at[0], at[1]] = master.astype(bf16)
            stores.append(
                pltpu.make_async_copy(
                    r.grad.at[which, s], grad_out.at[at], r.out_sem.at[which, s]
                )
            )
            stores[-1].start()

    def yc_copy(k):
        return send(
            r.y_part.at[k, :, other],
            r.y_core.at[k],
            r.yc_ss.at[k],
            r.yc_rs.at[k],
            device(x, y, z, other),
        )

    def yx_copy(k):
        return send(
            r.yx_send.at[k - 1],
            r.yx_recv.at[k - 1],
            r.yx_ss.at[k - 1],
            r.yx_rs.at[k - 1],
            device((x + NX - k) % NX, y, z, core),
        )

    for k in (2, 1, 3, 0):
        inputs = r.x_own[...] if k == 0 else r.xx_recv[k - 1]
        product = jnp.dot(
            inputs.reshape(NZ * 16, rows), r.rollout[...], preferred_element_type=f32
        )
        r.y_part[k] = product.reshape(NZ, 2, 8, columns)
        yc_copy(k).start()
    for k in (2, 1, 3):
        yc_copy(k).wait()
        r.yx_send[k - 1] = r.y_part[k, :, core] + r.y_core[k]
        yx_copy(k).start()
    yc_copy(0).wait()
    r.y_sum[...] = r.y_part[0, :, core] + r.y_core[0]
    for unit in range(UNITS):
        away, _ = unit_place(unit)

        @pl.when(jnp.logical_or(x != y, away != 0))
        def _():
            t_copy(unit).wait_send()

    for k in (1, 3, 2):
        yx_copy(k).wait()
        r.y_sum[...] += r.yx_recv[k - 1]

    def yz_copy(k):
        return send(
            r.y_sum.at[(z + k) % NZ],
            r.yz_recv.at[k - 1],
            r.yz_sem.at[0],
            r.yz_sem.at[1],
            device(x, y, (z + k) % NZ, core),
        )

    for k in (4, 3, 5, 2, 6, 1, 7):
        yz_copy(k).start()
    for store in stores:
        store.wait()
    send(
        r.y_sum.at[pl.ds(0, NZ - 1)],
        r.yz_recv,
        r.yz_sem.at[0],
        r.yz_sem.at[1],
        device(x, y, (z + 1) % NZ, core),
    ).wait()
    fresh = r.y_sum[z]
    for k in range(NZ - 1):
        fresh = fresh + r.yz_recv[k]
    for s in range(4):
        new_out[s] = fresh[2 * s : 2 * s + 2].astype(bf16)
    fresh = fresh.astype(bf16)

    line = lax.broadcasted_iota(jnp.int32, (64, 8), 0)
    spot = lax.broadcasted_iota(jnp.int32, (64, 8), 1)
    allowed = jnp.logical_and((line // 8) % 2 == spot % 2, spot // 2 <= line // 16)
    for kv_head in range(2):
        key = fresh[:, kv_head * 2 * head : (kv_head * 2 + 1) * head]
        value = fresh[:, (kv_head * 2 + 1) * head : (kv_head * 2 + 2) * head]
        score = lax.dot_general(
            r.query[kv_head].reshape(64, head).astype(bf16), key, (((1,), (1,)), ((), ())), preferred_element_type=f32
        )
        score = jnp.where(allowed, score * scale, -jnp.inf)
        before = r.top[kv_head][:, :1]
        highest = jnp.maximum(before, jnp.max(score, axis=1, keepdims=True))
        weight = jnp.exp(score - highest)
        factor = jnp.exp(before - highest)
        total = r.total[kv_head][:, :1] * factor + jnp.sum(weight, axis=1, keepdims=True)
        result = r.att[kv_head] * factor + jnp.dot(
            weight.astype(bf16), value, preferred_element_type=f32
        )
        r.answer[kv_head] = (result / total).reshape(8, 8, head)
        for g in range(8):
            value = r.answer[kv_head, :, g, :]
            at = pl.ds((kv_head * 8 + g) * head, head)
            for s in range(4):
                att_out[s, :, at] = value[2 * s : 2 * s + 2].astype(bf16)


def shards(
    features,
    kv_cotangent,
    master_weight,
    first_moment,
    second_moment,
    decode_inputs,
    queries,
    kv_cache,
    cache_lengths,
):
    tokens = features.shape[0]
    rows, columns = master_weight.shape
    steps, own_rows, width = decode_inputs.shape
    heads, slots, head = kv_cache.shape[2:]
    shapes = scratch(rows, columns, tokens, slots, head)
    in_vmem = pl.BlockSpec(memory_space=pltpu.VMEM)
    anywhere = pl.BlockSpec(memory_space=pl.ANY)
    gradient, new_kv, attended = pl.pallas_call(
        functools.partial(kernel, tuple(shapes)),
        out_shape=(
            jax.ShapeDtypeStruct((rows, columns), f32),
            jax.ShapeDtypeStruct((steps, own_rows, columns), bf16),
            jax.ShapeDtypeStruct(queries.shape, bf16),
        ),
        in_specs=[pl.BlockSpec(memory_space=pltpu.SMEM), in_vmem, in_vmem] + [anywhere] * 6,
        out_specs=(anywhere, in_vmem, in_vmem),
        scratch_shapes=list(shapes.values()),
        compiler_params=pltpu.CompilerParams(
            collective_id=0, has_side_effects=True, vmem_limit_bytes=56 * 2**20
        ),
        name="fused_step",
    )(
        cache_lengths,
        queries,
        decode_inputs,
        features,
        kv_cotangent,
        master_weight,
        first_moment,
        second_moment,
        kv_cache,
    )
    state = adam(gradient, master_weight, first_moment, second_moment)
    return (*state, new_kv, attended)


def solution(mesh):
    in_specs = (
        P(("learn", "dp"), "tp"),
        P(("learn", "dp"), "tp"),
        P(("learn", "dp"), "tp"),
        P(("learn", "dp"), "tp"),
        P(("learn", "dp"), "tp"),
        P(None, ("learn", "dp"), None),
        P(None, ("learn", "dp"), "tp"),
        P(None, ("learn", "dp"), "tp", None, None),
        P(("learn", "dp")),
    )
    out_specs = (
        P(("learn", "dp"), "tp"),
        P(("learn", "dp"), "tp"),
        P(("learn", "dp"), "tp"),
        P(None, ("learn", "dp"), "tp"),
        P(None, ("learn", "dp"), "tp"),
    )
    return jax.shard_map(shards, mesh=mesh, in_specs=in_specs, out_specs=out_specs, check_vma=False)
```

```python
import functools
import types

import jax
import jax.numpy as jnp
from jax import lax
from jax.experimental import pallas as pl
from jax.experimental.pallas import tpu as pltpu
from jax.sharding import PartitionSpec as P

learn_rate = 0.005
decay_rate = 0.1
first_fix = 1.0 - 0.9**10
second_fix = 1.0 - 0.999**10

MESH = pl.DeviceIdType.MESH
UNITS = 8
NX, NY, NZ = 4, 4, 8
NEW = 'P'
PLACES = ((0, 0), (0, 1), (1, 0), (3, 0), (2, 0), (1, 1), (3, 1), (2, 1))
Z_UNITS = (1, 3, 6, 7)
ORDER = (
    "B0", "B1", "X0", "C0", "D0", "C1", "D1", "Y0", "A0", "F0", "B2", "E0",
    "I1", "B3", "C2", "A1", "G0", "F1", "D2", "B5", "J1", "B6", "C3", "D3",
    "C5", "D5", "C6", "E2", "H0", "K1", "D6", "B4", "B7", "I3", "C4", "E5",
    "A2", "G2", "L1", "D4", "C7", "J3", "I6", "D7", "A3", "G5", "H2", "E4",
    "K3", "I7", "J6", "G4", "H5", "J7", "K6", "L3", "K7", "H4", "L6", "P0",
    "L7", "Q0", "P1", "Q1", "R0", "R1", "S0", "S1",
)

bf16 = jnp.bfloat16
f32 = jnp.float32


def position():
    learn, dp = lax.axis_index("learn"), lax.axis_index("dp")
    return learn // 4, lax.axis_index("tp"), (learn % 4) * 2 + dp // 2, dp % 2


def device(x, y, z, core):
    return {"learn": x * 4 + z // 2, "tp": y, "dp": (z % 2) * 2 + core}


def send(source, target, send_sem, recv_sem, where):
    return pltpu.make_async_remote_copy(
        src_ref=source,
        dst_ref=target,
        send_sem=send_sem,
        recv_sem=recv_sem,
        device_id=where,
        device_id_type=MESH,
    )


def adam(gradient, master, first, second):
    first = 0.9 * first + 0.1 * gradient
    second = 0.999 * second + 0.001 * gradient * gradient
    update = (first / first_fix) / (jnp.sqrt(second / second_fix) + 1e-08)
    return master - learn_rate * (update + decay_rate * master), first, second


def scratch(rows, columns, tokens, slots, head):
    part, half = rows // 4, columns // 2
    dma = pltpu.SemaphoreType.DMA
    return dict(
        feat=pltpu.VMEM((tokens, 16 * rows), bf16),
        turned=pltpu.VMEM((2, NZ, rows, tokens), bf16),
        cot=pltpu.VMEM((UNITS, tokens, half), bf16),
        core_send=pltpu.VMEM((UNITS, NZ, 4, part, half), bf16),
        core_recv=pltpu.VMEM((UNITS, NZ, 4, part, half), bf16),
        mine=pltpu.VMEM((NZ, 4, part, half), f32),
        keep=pltpu.VMEM((UNITS, 2, 2, 4, part, half), f32),
        x1_send=pltpu.VMEM((UNITS, 2, 2, 4, part, half), bf16),
        x1_recv=pltpu.VMEM((UNITS, 2, 2, 4, part, half), bf16),
        x2_send=pltpu.VMEM((UNITS, 2, 4, part, half), bf16),
        x2_recv=pltpu.VMEM((UNITS, 2, 4, part, half), bf16),
        a_send=pltpu.VMEM((len(Z_UNITS), 2, 2, 4, part, half), bf16),
        a_recv=pltpu.VMEM((len(Z_UNITS), 2, 2, 4, part, half), bf16),
        a_keep=pltpu.VMEM((len(Z_UNITS), 2, 2, 4, part, half), f32),
        b_keep=pltpu.VMEM((len(Z_UNITS), 2, 2, 2, part, half), f32),
        b_send=pltpu.VMEM((len(Z_UNITS), 2, 2, 2, part, half), bf16),
        b_recv=pltpu.VMEM((len(Z_UNITS), 2, 2, 2, part, half), bf16),
        c_send=pltpu.VMEM((len(Z_UNITS), 2, 2, part, half), bf16),
        c_recv=pltpu.VMEM((len(Z_UNITS), 2, 2, part, half), bf16),
        d_sum=pltpu.VMEM((4, part, half), f32),
        d_send=pltpu.VMEM((len(Z_UNITS), 3, part, half), bf16),
        d_recv=pltpu.VMEM((len(Z_UNITS), 3, part, half), bf16),
        a_ss=dma((len(Z_UNITS), 2)),
        a_rs=dma((len(Z_UNITS), 2)),
        b_ss=dma((len(Z_UNITS), 2)),
        b_rs=dma((len(Z_UNITS), 2)),
        c_ss=dma((len(Z_UNITS), 2)),
        c_rs=dma((len(Z_UNITS), 2)),
        d_ss=dma((len(Z_UNITS),)),
        d_rs=dma((len(Z_UNITS),)),
        z_sum=pltpu.VMEM((NZ, part, half), f32),
        z_own=pltpu.VMEM((UNITS, part, half), f32),
        z_send=pltpu.VMEM((UNITS, NZ - 1, part, half), bf16),
        z_recv=pltpu.VMEM((UNITS, NZ - 1, part, half), bf16),
        t_send=pltpu.VMEM((UNITS, part, half), f32),
        grad=pltpu.VMEM((2, 4, part, half), f32),
        kv=pltpu.VMEM((2, 2, 2, slots, head), bf16),
        state=pltpu.VMEM((3, rows, columns), f32),
        rollout=pltpu.VMEM((rows, columns), bf16),
        x_mine=pltpu.VMEM((2, 32, 8, rows), f32),
        x_pair=pltpu.VMEM((32, 8, rows), f32),
        xz_send=pltpu.VMEM((NZ - 1, NX, 16, rows), bf16),
        xz_recv=pltpu.VMEM((NZ - 1, NX, 16, rows), bf16),
        xx_send=pltpu.VMEM((NX - 1, NZ, 16, rows), bf16),
        xx_recv=pltpu.VMEM((NX - 1, NZ, 16, rows), bf16),
        xx_own=pltpu.VMEM((NZ, 16, rows), bf16),
        x_all=pltpu.VMEM((NX, NZ, 16, rows), bf16),
        y_part=pltpu.VMEM((2, NX, NZ, 2, 8, half), f32),
        y_core=pltpu.VMEM((2, NX, NZ, 8, half), f32),
        yx_send=pltpu.VMEM((2, NX - 1, NZ, 8, half), f32),
        yx_recv=pltpu.VMEM((2, NX - 1, NZ, 8, half), f32),
        y_sum=pltpu.VMEM((2, NZ, 8, half), f32),
        yz_recv=pltpu.VMEM((2, NZ - 1, 8, half), f32),
        scores=pltpu.VMEM((32, slots), f32),
        query=pltpu.VMEM((2, 8, 8, head), f32),
        answer=pltpu.VMEM((2, 8, 8, head), f32),
        att=pltpu.VMEM((2, 64, head), f32),
        top=pltpu.VMEM((2, 64, head), f32),
        total=pltpu.VMEM((2, 64, head), f32),
        load_sem=dma((7,)),
        out_sem=dma((2, 4)),
        cot_ss=dma((6,)),
        cot_rs=dma((UNITS,)),
        core_ss=dma((UNITS,)),
        core_rs=dma((UNITS,)),
        x1_ss=dma((UNITS, 2)),
        x1_rs=dma((UNITS, 2)),
        x2_ss=dma((UNITS, 2)),
        x2_rs=dma((UNITS, 2)),
        z_ss=dma((UNITS,)),
        z_rs=dma((UNITS,)),
        t_ss=dma((UNITS,)),
        t_rs=dma((2, 4)),
        xc_sem=dma((2,)),
        xz_sem=dma((2,)),
        xx_ss=dma((3,)),
        xx_rs=dma((3,)),
        yc_ss=dma((2, 4)),
        yc_rs=dma((2, 4)),
        yx_ss=dma((2, 3)),
        yx_rs=dma((2, 3)),
        yz_sem=dma((2, 2)),
    )


def kernel(names, *refs):
    (lengths, q_ref, x_ref, f_hbm, c_hbm, w_hbm, m_hbm, v_hbm, kv_hbm) = refs[:9]
    (grad_out, new_out, att_out) = refs[9:12]
    r = types.SimpleNamespace(**dict(zip(names, refs[12:])))
    x, y, z, core = position()
    other = 1 - core
    flip, mirror = x + 1 - 2 * (x % 2), 3 - x
    first_partner, second_partner = (flip, mirror), (mirror, flip)
    rows, columns = r.rollout.shape
    part, half = rows // 4, columns // 2
    tokens = r.feat.shape[0]
    slots, head = r.kv.shape[3:]
    scale = head**-0.5

    loads = [
        pltpu.make_async_copy(source, target, r.load_sem.at[i])
        for i, (source, target) in enumerate(
            (
                (c_hbm.at[:, pl.ds(0, half)], r.cot.at[0]),
                (f_hbm, r.feat),
                (c_hbm.at[:, pl.ds(half, half)], r.cot.at[1]),
                (kv_hbm, r.kv),
                (w_hbm, r.state.at[0]),
                (m_hbm, r.state.at[1]),
                (v_hbm, r.state.at[2]),
            )
        )
    ]
    for load in loads[:3]:
        load.start()

    inputs = jnp.concatenate([x_ref[s].astype(f32) for s in range(4)], axis=0)
    for block in range(64):
        r.x_mine[block % 2, block // 2] = inputs[:, block * rows : (block + 1) * rows]

    barrier = pltpu.get_barrier_semaphore()

    def greet(where):
        pl.semaphore_signal(barrier, inc=1, device_id=where, device_id_type=MESH)

    greet(device(x, y, z, other))
    for k in range(1, NX):
        greet(device((x + k) % NX, y, z, core))
    for k in range(1, NZ):
        greet(device(x, y, (z + k) % NZ, core))
    for k in range(1, NY):
        greet(device(x, (y + k) % NY, z, core))
    for k in range(4):

        @pl.when(jnp.logical_or(x != y, y != k))
        def _():
            greet(device(y, k, z, core))

        @pl.when(jnp.logical_or(x != y, x != k))
        def _():
            greet(device(k, x, z, core))

    same = (4 - (x - y + 4) % 4) // 4
    pl.semaphore_wait(barrier, 1 + (NX - 1) + (NZ - 1) + (NY - 1) + 8 - 2 * same)

    slot = {place: unit for unit, place in enumerate(PLACES)}
    arrived = {slot[0, 0], slot[0, 1]}

    def cot_copy(index):
        step = (3, 1, 3, 1, 1, 3)[index]
        half_of = (0, 0, 1, 1, 0, 1)[index]
        source = slot[0, half_of] if index < 4 else slot[(3, 1)[half_of], half_of]
        target = slot[4 - step, half_of] if index < 4 else slot[2, half_of]
        return send(
            r.cot.at[source],
            r.cot.at[target],
            r.cot_ss.at[index],
            r.cot_rs.at[target],
            device(x, (y + step) % NY, z, core),
        )

    def have(unit):
        if unit not in arrived:
            arrived.add(unit)
            send(
                r.cot.at[unit],
                r.cot.at[unit],
                r.cot_ss.at[0],
                r.cot_rs.at[unit],
                device(x, (y + 1) % NY, z, core),
            ).wait_recv()

    def forward(part_of):
        have(slot[(3, 1)[part_of], part_of])
        cot_copy(4 + part_of).start()

    x_swap = send(
        r.x_mine.at[other],
        r.x_pair,
        r.xc_sem.at[0],
        r.xc_sem.at[1],
        device(x, y, z, other),
    )
    x_swap.start()
    loads[0].wait()
    for index in range(2):
        cot_copy(index).start()
    loads[2].wait()
    for index in range(2, 4):
        cot_copy(index).start()
    loads[1].wait()
    for load in loads[3:]:
        load.start()

    def turn(side):
        for row_block in range(NZ):
            columns_of = pl.ds(pl.multiple_of((row_block * 2 + side) * rows, rows), rows)
            r.turned[side, row_block] = r.feat[:, columns_of].T

    def multiply(side, unit, store):
        def step(i, carry):
            left = r.turned[side, pl.ds(2 * i, 2)].reshape(2 * rows, tokens)
            product = jnp.dot(left, r.cot[unit], preferred_element_type=f32)
            store(i, product.reshape(2, 4, part, half))
            return carry

        lax.fori_loop(0, NZ // 2, step, 0)

    def core_copy(unit):
        return send(
            r.core_send.at[unit],
            r.core_recv.at[unit],
            r.core_ss.at[unit],
            r.core_rs.at[unit],
            device(x, y, z, other),
        )

    def x1_copy(unit, side):
        return send(
            r.x1_send.at[unit, side],
            r.x1_recv.at[unit, side],
            r.x1_ss.at[unit, side],
            r.x1_rs.at[unit, side],
            device(first_partner[side], y, z, core),
        )

    def x2_copy(unit, side):
        return send(
            r.x2_send.at[unit, side],
            r.x2_recv.at[unit, side],
            r.x2_ss.at[unit, side],
            r.x2_rs.at[unit, side],
            device(second_partner[side], y, z, core),
        )

    def z_copy(unit, k):
        return send(
            r.z_send.at[unit, k - 1],
            r.z_recv.at[unit, k - 1],
            r.z_ss.at[unit],
            r.z_rs.at[unit],
            device(x, y, (z + k) % NZ, core),
        )

    def z_all(unit):
        return send(
            r.z_send.at[unit],
            r.z_recv.at[unit],
            r.z_ss.at[unit],
            r.z_rs.at[unit],
            device(x, y, (z + 1) % NZ, core),
        )

    def t_copy(unit):
        away, which = PLACES[unit]
        return send(
            r.t_send.at[unit],
            r.grad.at[which, x],
            r.t_ss.at[unit],
            r.t_rs.at[which, x],
            device(y, (y + away) % NY, z, core),
        )

    def stage0(unit):
        have(unit)

        def store(i, product):
            r.core_send[unit, pl.ds(2 * i, 2)] = product.astype(bf16)

        multiply(other, unit, store)
        core_copy(unit).start()

    def own(unit):
        if unit == 0:
            turn(core)

        def store(i, product):
            r.mine[pl.ds(2 * i, 2)] = product

        multiply(core, unit, store)

    def stage1(unit):
        core_copy(unit).wait()
        if unit in Z_UNITS:
            at_unit = Z_UNITS.index(unit)
            for side in range(2):
                for at in range(2):
                    block = 2 * (2 * side + at) + 1 - z % 2
                    r.a_send[at_unit, side, at] = (
                        r.mine[block] + r.core_recv[unit, block].astype(f32)
                    ).astype(bf16)
                a_copy(unit, side).start()
            for side in range(2):
                for at in range(2):
                    block = 2 * (2 * side + at) + z % 2
                    r.a_keep[at_unit, side, at] = r.mine[block] + r.core_recv[
                        unit, block
                    ].astype(f32)

        else:
            for side in range(2):
                partner = first_partner[side]
                away = (partner, (3 - partner, partner + 1 - 2 * (partner % 2))[side])
                for k in range(2):
                    for at in range(4):
                        row_block = side * 4 + at
                        r.x1_send[unit, side, k, at] = (
                            r.mine[row_block, away[k]]
                            + r.core_recv[unit, row_block, away[k]].astype(f32)
                        ).astype(bf16)
                x1_copy(unit, side).start()
            for side in range(2):
                near = (x, second_partner[side])
                for k in range(2):
                    for at in range(4):
                        row_block = side * 4 + at
                        r.keep[unit, side, k, at] = r.mine[row_block, near[k]] + r.core_recv[
                            unit, row_block, near[k]
                        ].astype(f32)

    def a_copy(unit, side):
        return send(
            r.a_send.at[Z_UNITS.index(unit), side],
            r.a_recv.at[Z_UNITS.index(unit), side],
            r.a_ss.at[Z_UNITS.index(unit), side],
            r.a_rs.at[Z_UNITS.index(unit), side],
            device(x, y, (z + 1 - 2 * (z % 2), (z + 7 + 2 * (z % 2)) % NZ)[side], core),
        )

    def b_copy(unit, side):
        return send(
            r.b_send.at[Z_UNITS.index(unit), side],
            r.b_recv.at[Z_UNITS.index(unit), side],
            r.b_ss.at[Z_UNITS.index(unit), side],
            r.b_rs.at[Z_UNITS.index(unit), side],
            device(first_partner[side], y, z, core),
        )

    def c_copy(unit, side):
        return send(
            r.c_send.at[Z_UNITS.index(unit), side],
            r.c_recv.at[Z_UNITS.index(unit), side],
            r.c_ss.at[Z_UNITS.index(unit), side],
            r.c_rs.at[Z_UNITS.index(unit), side],
            device(second_partner[side], y, z, core),
        )

    def d_copy(unit, k):
        return send(
            r.d_send.at[Z_UNITS.index(unit), k - 1],
            r.d_recv.at[Z_UNITS.index(unit), k - 1],
            r.d_ss.at[Z_UNITS.index(unit)],
            r.d_rs.at[Z_UNITS.index(unit)],
            device(x, y, (z + 2 * k) % NZ, core),
        )

    def d_all(unit):
        return send(
            r.d_send.at[Z_UNITS.index(unit)],
            r.d_recv.at[Z_UNITS.index(unit)],
            r.d_ss.at[Z_UNITS.index(unit)],
            r.d_rs.at[Z_UNITS.index(unit)],
            device(x, y, (z + 2) % NZ, core),
        )

    def away_and_near(side):
        partner = first_partner[side]
        away = (partner, (3 - partner, partner + 1 - 2 * (partner % 2))[side])
        return away, (x, second_partner[side])

    def z_stage2(unit):
        at_unit = Z_UNITS.index(unit)
        for side in range(2):
            a_copy(unit, side).wait()
            away, near = away_and_near(side)
            for k in range(2):
                for at in range(2):
                    r.b_send[at_unit, side, k, at] = (
                        r.a_keep[at_unit, side, at, away[k]]
                        + r.a_recv[at_unit, side, at, away[k]].astype(f32)
                    ).astype(bf16)
            b_copy(unit, side).start()
            for k in range(2):
                for at in range(2):
                    r.b_keep[at_unit, side, k, at] = r.a_keep[
                        at_unit, side, at, near[k]
                    ] + r.a_recv[at_unit, side, at, near[k]].astype(f32)

    def z_stage3(unit):
        at_unit = Z_UNITS.index(unit)
        for side in range(2):
            b_copy(unit, side).wait()
            r.c_send[at_unit, side] = (
                r.b_keep[at_unit, side, 1] + r.b_recv[at_unit, side, 1].astype(f32)
            ).astype(bf16)
            c_copy(unit, side).start()
            r.b_keep[at_unit, side, 0] += r.b_recv[at_unit, side, 0].astype(f32)

    def z_stage4(unit):
        at_unit = Z_UNITS.index(unit)
        for side in range(2):
            c_copy(unit, side).wait()
            for at in range(2):
                r.d_sum[side * 2 + at] = r.b_keep[at_unit, side, 0, at] + r.c_recv[
                    at_unit, side, at
                ].astype(f32)
        for k in (2, 1, 3):
            r.d_send[at_unit, k - 1] = r.d_sum[(z // 2 + k) % 4].astype(bf16)
            d_copy(unit, k).start()
        r.z_own[unit] = r.d_sum[z // 2]

    def z_stage5(unit):
        d_all(unit).wait()
        total = r.z_own[unit]
        for k in range(3):
            total = total + r.d_recv[Z_UNITS.index(unit), k].astype(f32)
        finish(unit, total)

    def stage2(unit):
        for side in range(2):
            x1_copy(unit, side).wait()
            r.x2_send[unit, side] = (
                r.keep[unit, side, 1] + r.x1_recv[unit, side, 1].astype(f32)
            ).astype(bf16)
            x2_copy(unit, side).start()
        for side in range(2):
            r.keep[unit, side, 0] += r.x1_recv[unit, side, 0].astype(f32)

    def stage3(unit):
        for side in range(2):
            x2_copy(unit, side).wait()
            for at in range(4):
                r.z_sum[side * 4 + at] = r.keep[unit, side, 0, at] + r.x2_recv[
                    unit, side, at
                ].astype(f32)
        for k in (4, 3, 5, 2, 6, 1, 7):
            r.z_send[unit, k - 1] = r.z_sum[(z + k) % NZ].astype(bf16)
            z_copy(unit, k).start()
        r.z_own[unit] = r.z_sum[z]

    def stage4(unit):
        z_all(unit).wait()
        total = r.z_own[unit]
        for k in range(NZ - 1):
            total = total + r.z_recv[unit, k].astype(f32)
        finish(unit, total)

    def finish(unit, total):
        away, which = PLACES[unit]

        def go():
            r.t_send[unit] = total
            t_copy(unit).start()

        if away == 0:

            @pl.when(x == y)
            def _():
                r.grad[which, x] = total

            pl.when(x != y)(go)
        else:
            go()

    def xx_copy(k):
        return send(
            r.xx_send.at[k - 1],
            r.xx_recv.at[k - 1],
            r.xx_ss.at[k - 1],
            r.xx_rs.at[k - 1],
            device((x + k) % NX, y, z, core),
        )

    def xz_copy(k, source, target):
        return send(
            source,
            target,
            r.xz_sem.at[0],
            r.xz_sem.at[1],
            device(x, y, (z + k) % NZ, core),
        )

    def spread_x(_):
        x_swap.wait()
        for k in (2, 1, 3, 0):
            target = r.xx_own if k == 0 else r.xx_send.at[k - 1]
            for block in range(NZ):
                at = (x + k) % NX * NZ + block
                mine, pair = r.x_mine[core, at], r.x_pair[at]
                low, high = jnp.where(core == 0, mine, pair), jnp.where(core == 0, pair, mine)
                target[block] = jnp.concatenate([low, high], axis=0).astype(bf16)
            if k > 0:
                xx_copy(k).start()

    def spread_z(_):
        for k in range(1, NX):
            xx_copy(k).wait()
        for k in (4, 3, 5, 2, 6, 1, 7):
            to = (z + k) % NZ
            r.xz_send[k - 1, 0] = r.xx_own[to]
            for j in range(1, NX):
                r.xz_send[k - 1, j] = r.xx_recv[j - 1, to]
            xz_copy(k, r.xz_send.at[k - 1], r.xz_recv.at[k - 1]).start()

    def spread_done():
        xz_copy(1, r.xz_send, r.xz_recv).wait()
        r.x_all[0, z] = r.xx_own[z]
        for j in range(1, NX):
            r.x_all[j, z] = r.xx_recv[j - 1, z]
        for k in range(1, NZ):
            for j in range(NX):
                r.x_all[j, (z + NZ - k) % NZ] = r.xz_recv[k - 1, j]
        for k in range(4, 7):
            loads[k].wait()

    chunk = min(1024, slots)

    def cached(pair):
        row, kv_head = pair // 2, pair % 2
        if pair == 0:
            loads[3].wait()
            asked = jnp.concatenate([q_ref[s].astype(f32) for s in range(4)], axis=0)
            for h in range(2):
                for g in range(8):
                    r.query[h, :, g, :] = asked[:, (h * 8 + g) * head : (h * 8 + g + 1) * head]
        query = r.query[kv_head].reshape(4, 2, 8, head)
        query = query[:, row].reshape(32, head).astype(bf16)

        def score(i, highest):
            at = pl.ds(pl.multiple_of(i * chunk, chunk), chunk)
            value = lax.dot_general(
                query,
                r.kv[0, row, kv_head, at],
                (((1,), (1,)), ((), ())),
                preferred_element_type=f32,
            )
            places = i * chunk + lax.broadcasted_iota(jnp.int32, value.shape, 1)
            value = jnp.where(places < lengths[row], value * scale, -jnp.inf)
            r.scores[:, at] = value
            return jnp.maximum(highest, jnp.max(value, axis=1, keepdims=True))

        highest = lax.fori_loop(0, slots // chunk, score, jnp.full((32, 1), -jnp.inf, f32))

        def weigh(i, carry):
            total, result = carry
            at = pl.ds(pl.multiple_of(i * chunk, chunk), chunk)
            weight = jnp.exp(r.scores[:, at] - highest)
            total = total + jnp.sum(weight, axis=1, keepdims=True)
            result = result + jnp.dot(
                weight.astype(bf16), r.kv[1, row, kv_head, at], preferred_element_type=f32
            )
            return total, result

        total, result = lax.fori_loop(
            0, slots // chunk, weigh, (jnp.zeros((32, 1), f32), jnp.zeros((32, head), f32))
        )
        highest = jnp.broadcast_to(highest, (32, head))
        total = jnp.broadcast_to(total, (32, head))
        for s in range(4):
            at = pl.ds(s * 16 + row * 8, 8)
            one = slice(s * 8, s * 8 + 8)
            r.att[kv_head, at] = result[one]
            r.top[kv_head, at] = highest[one]
            r.total[kv_head, at] = total[one]

    def store_copy(which, s):
        return pltpu.make_async_copy(
            r.grad.at[which, s],
            grad_out.at[pl.ds(s * part, part), pl.ds(which * half, half)],
            r.out_sem.at[which, s],
        )

    def yc_copy(which, k):
        return send(
            r.y_part.at[which, k, :, other],
            r.y_core.at[which, k],
            r.yc_ss.at[which, k],
            r.yc_rs.at[which, k],
            device(x, y, z, other),
        )

    def yx_copy(which, k):
        return send(
            r.yx_send.at[which, k - 1],
            r.yx_recv.at[which, k - 1],
            r.yx_ss.at[which, k - 1],
            r.yx_rs.at[which, k - 1],
            device((x + NX - k) % NX, y, z, core),
        )

    def yz_copy(which, k):
        return send(
            r.y_sum.at[which, (z + k) % NZ],
            r.yz_recv.at[which, k - 1],
            r.yz_sem.at[which, 0],
            r.yz_sem.at[which, 1],
            device(x, y, (z + k) % NZ, core),
        )

    def new0(which):
        if which == first_head:
            spread_done()
        for s in range(4):

            @pl.when(jnp.logical_or(x != y, x != s))
            def _():
                send(
                    r.t_send.at[0],
                    r.grad.at[which, s],
                    r.t_ss.at[0],
                    r.t_rs.at[which, s],
                    device(x, (y + 1) % NY, z, core),
                ).wait_recv()

            at = (pl.ds(s * part, part), pl.ds(which * half, half))
            master, _, _ = adam(r.grad[which, s], *(r.state[i, at[0], at[1]] for i in range(3)))
            r.rollout[at[0], at[1]] = master.astype(bf16)
        for k in (2, 1, 3, 0):
            product = jnp.dot(
                r.x_all[k].reshape(NZ * 16, rows),
                r.rollout[:, which * half : (which + 1) * half],
                preferred_element_type=f32,
            )
            r.y_part[which, k] = product.reshape(NZ, 2, 8, half)
            yc_copy(which, k).start()
        for s in range(4):
            store_copy(which, s).start()

    def new1(which):
        for k in (2, 1, 3):
            yc_copy(which, k).wait()
            r.yx_send[which, k - 1] = r.y_part[which, k, :, core] + r.y_core[which, k]
            yx_copy(which, k).start()
        yc_copy(which, 0).wait()
        r.y_sum[which] = r.y_part[which, 0, :, core] + r.y_core[which, 0]

    def new2(which):
        for k in (1, 3, 2):
            yx_copy(which, k).wait()
            r.y_sum[which] += r.yx_recv[which, k - 1]
        for k in (4, 3, 5, 2, 6, 1, 7):
            yz_copy(which, k).start()

    def new3(which):
        send(
            r.y_sum.at[which, pl.ds(0, NZ - 1)],
            r.yz_recv.at[which],
            r.yz_sem.at[which, 0],
            r.yz_sem.at[which, 1],
            device(x, y, (z + 1) % NZ, core),
        ).wait()
        fresh = r.y_sum[which, z]
        for k in range(NZ - 1):
            fresh = fresh + r.yz_recv[which, k]
        for s in range(4):
            new_out[s, :, pl.ds(which * half, half)] = fresh[2 * s : 2 * s + 2].astype(bf16)
        fresh = fresh.astype(bf16)
        key, value = fresh[:, :head], fresh[:, head:]
        line = lax.broadcasted_iota(jnp.int32, (64, 8), 0)
        spot = lax.broadcasted_iota(jnp.int32, (64, 8), 1)
        allowed = jnp.logical_and((line // 8) % 2 == spot % 2, spot // 2 <= line // 16)
        score = lax.dot_general(
            r.query[which].reshape(64, head).astype(bf16),
            key,
            (((1,), (1,)), ((), ())),
            preferred_element_type=f32,
        )
        score = jnp.where(allowed, score * scale, -jnp.inf)
        before = r.top[which][:, :1]
        highest = jnp.maximum(before, jnp.max(score, axis=1, keepdims=True))
        weight = jnp.exp(score - highest)
        factor = jnp.exp(before - highest)
        total = r.total[which][:, :1] * factor + jnp.sum(weight, axis=1, keepdims=True)
        result = r.att[which] * factor + jnp.dot(
            weight.astype(bf16), value, preferred_element_type=f32
        )
        r.answer[which] = (result / total).reshape(8, 8, head)
        for g in range(8):
            value = r.answer[which, :, g, :]
            at = pl.ds((which * 8 + g) * head, head)
            for s in range(4):
                att_out[s, :, at] = value[2 * s : 2 * s + 2].astype(bf16)

    steps = dict(
        F=forward,
        X=spread_x,
        Y=spread_z,
        A=cached,
        B=stage0,
        C=own,
        D=stage1,
        E=stage2,
        G=stage3,
        H=stage4,
        I=z_stage2,
        J=z_stage3,
        K=z_stage4,
        L=z_stage5,
        P=new0,
        Q=new1,
        R=new2,
        S=new3,
    )
    order = [(word[0], int(word[1])) for word in ORDER]
    first_head = [place for name, place in order if name == NEW][0]
    turn(other)
    for name, place in order:
        steps[name](place)
    for unit in range(UNITS):
        if PLACES[unit][0] == 0:
            pl.when(x != y)(lambda: t_copy(unit).wait_send())
        else:
            t_copy(unit).wait_send()
    for index in range(6):
        cot_copy(index).wait_send()
    for which in range(2):
        for s in range(4):
            store_copy(which, s).wait()


def last(gradient, master, first, second, new_kv, attended, *results):
    values = (*adam(gradient[...], master[...], first[...], second[...]), new_kv[...], attended[...])
    for result, value in zip(results, values):
        result[...] = value


def shards(
    features,
    kv_cotangent,
    master_weight,
    first_moment,
    second_moment,
    decode_inputs,
    queries,
    kv_cache,
    cache_lengths,
):
    tokens = features.shape[0]
    rows, columns = master_weight.shape
    steps, own_rows, width = decode_inputs.shape
    heads, slots, head = kv_cache.shape[2:]
    shapes = scratch(rows, columns, tokens, slots, head)
    in_vmem = pl.BlockSpec(memory_space=pltpu.VMEM)
    anywhere = pl.BlockSpec(memory_space=pl.ANY)
    gradient, new_kv, attended = pl.pallas_call(
        functools.partial(kernel, tuple(shapes)),
        out_shape=(
            jax.ShapeDtypeStruct((rows, columns), f32),
            jax.ShapeDtypeStruct((steps, own_rows, columns), bf16),
            jax.ShapeDtypeStruct(queries.shape, bf16),
        ),
        in_specs=[pl.BlockSpec(memory_space=pltpu.SMEM), in_vmem, in_vmem] + [anywhere] * 6,
        out_specs=(anywhere, in_vmem, in_vmem),
        scratch_shapes=list(shapes.values()),
        compiler_params=pltpu.CompilerParams(
            collective_id=0, has_side_effects=True, vmem_limit_bytes=56 * 2**20
        ),
        name="fused_step",
    )(
        cache_lengths,
        queries,
        decode_inputs,
        features,
        kv_cotangent,
        master_weight,
        first_moment,
        second_moment,
        kv_cache,
    )
    like = jax.ShapeDtypeStruct((rows, columns), f32)
    return pl.pallas_call(
        last,
        out_shape=(
            like,
            like,
            like,
            jax.ShapeDtypeStruct(new_kv.shape, bf16),
            jax.ShapeDtypeStruct(attended.shape, bf16),
        ),
        in_specs=[in_vmem] * 6,
        out_specs=[in_vmem] * 5,
        name="last",
    )(gradient, master_weight, first_moment, second_moment, new_kv, attended)


def solution(mesh):
    in_specs = (
        P(("learn", "dp"), "tp"),
        P(("learn", "dp"), "tp"),
        P(("learn", "dp"), "tp"),
        P(("learn", "dp"), "tp"),
        P(("learn", "dp"), "tp"),
        P(None, ("learn", "dp"), None),
        P(None, ("learn", "dp"), "tp"),
        P(None, ("learn", "dp"), "tp", None, None),
        P(("learn", "dp")),
    )
    out_specs = (
        P(("learn", "dp"), "tp"),
        P(("learn", "dp"), "tp"),
        P(("learn", "dp"), "tp"),
        P(None, ("learn", "dp"), "tp"),
        P(None, ("learn", "dp"), "tp"),
    )
    return jax.shard_map(shards, mesh=mesh, in_specs=in_specs, out_specs=out_specs, check_vma=False)
```

```python
import functools
import types

import jax
import jax.numpy as jnp
from jax import lax
from jax.experimental import pallas as pl
from jax.experimental.pallas import tpu as pltpu
from jax.sharding import PartitionSpec as P

learn_rate = 0.005
decay_rate = 0.1
first_fix = 1.0 - 0.9**10
second_fix = 1.0 - 0.999**10

MESH = pl.DeviceIdType.MESH
UNITS = 8
NX, NY, NZ = 4, 4, 8
NEW = 'P'
PLACES = ((0, 0), (0, 1), (1, 0), (3, 0), (1, 1), (3, 1), (2, 0), (2, 1))
Z_UNITS = (1, 2, 4, 6, 7)
ORDER = (
    "B0", "B1", "X0", "C0", "D0", "C1", "D1", "Y0", "A0", "F0", "B2", "B3",
    "E0", "C2", "A1", "I1", "D2", "C3", "F1", "G0", "B4", "B5", "D3", "C4",
    "J1", "A2", "I2", "D4", "B6", "C5", "D5", "C6", "E3", "K1", "B7", "H0",
    "D6", "J2", "C7", "I4", "A3", "D7", "E5", "L1", "G3", "K2", "I6", "J4",
    "I7", "G5", "J6", "K4", "J7", "H3", "K6", "L2", "K7", "H5", "L4", "L6",
    "L7", "P0", "P1", "Q0", "Q1", "R0", "R1", "S0", "S1",
)

bf16 = jnp.bfloat16
f32 = jnp.float32


def position():
    learn, dp = lax.axis_index("learn"), lax.axis_index("dp")
    return learn // 4, lax.axis_index("tp"), (learn % 4) * 2 + dp // 2, dp % 2


def device(x, y, z, core):
    return {"learn": x * 4 + z // 2, "tp": y, "dp": (z % 2) * 2 + core}


def send(source, target, send_sem, recv_sem, where):
    return pltpu.make_async_remote_copy(
        src_ref=source,
        dst_ref=target,
        send_sem=send_sem,
        recv_sem=recv_sem,
        device_id=where,
        device_id_type=MESH,
    )


def adam(gradient, master, first, second):
    first = 0.9 * first + 0.1 * gradient
    second = 0.999 * second + 0.001 * gradient * gradient
    update = (first / first_fix) / (jnp.sqrt(second / second_fix) + 1e-08)
    return master - learn_rate * (update + decay_rate * master), first, second


def scratch(rows, columns, tokens, slots, head):
    part, half = rows // 4, columns // 2
    dma = pltpu.SemaphoreType.DMA
    return dict(
        feat=pltpu.VMEM((tokens, 16 * rows), bf16),
        turned=pltpu.VMEM((2, NZ, rows, tokens), bf16),
        cot=pltpu.VMEM((UNITS, tokens, half), bf16),
        core_send=pltpu.VMEM((UNITS, NZ, 4, part, half), bf16),
        core_recv=pltpu.VMEM((UNITS, NZ, 4, part, half), bf16),
        mine=pltpu.VMEM((NZ, 4, part, half), f32),
        keep=pltpu.VMEM((UNITS, 2, 2, 4, part, half), f32),
        x1_send=pltpu.VMEM((UNITS, 2, 2, 4, part, half), bf16),
        x1_recv=pltpu.VMEM((UNITS, 2, 2, 4, part, half), bf16),
        x2_send=pltpu.VMEM((UNITS, 2, 4, part, half), bf16),
        x2_recv=pltpu.VMEM((UNITS, 2, 4, part, half), bf16),
        a_send=pltpu.VMEM((max(1, len(Z_UNITS)), 2, 2, 4, part, half), bf16),
        a_recv=pltpu.VMEM((max(1, len(Z_UNITS)), 2, 2, 4, part, half), bf16),
        a_keep=pltpu.VMEM((max(1, len(Z_UNITS)), 2, 2, 4, part, half), f32),
        b_keep=pltpu.VMEM((max(1, len(Z_UNITS)), 2, 2, 2, part, half), f32),
        b_send=pltpu.VMEM((max(1, len(Z_UNITS)), 2, 2, 2, part, half), bf16),
        b_recv=pltpu.VMEM((max(1, len(Z_UNITS)), 2, 2, 2, part, half), bf16),
        c_send=pltpu.VMEM((max(1, len(Z_UNITS)), 2, 2, part, half), bf16),
        c_recv=pltpu.VMEM((max(1, len(Z_UNITS)), 2, 2, part, half), bf16),
        d_sum=pltpu.VMEM((4, part, half), f32),
        d_send=pltpu.VMEM((max(1, len(Z_UNITS)), 3, part, half), bf16),
        d_recv=pltpu.VMEM((max(1, len(Z_UNITS)), 3, part, half), bf16),
        a_ss=dma((max(1, len(Z_UNITS)), 2)),
        a_rs=dma((max(1, len(Z_UNITS)), 2)),
        b_ss=dma((max(1, len(Z_UNITS)), 2)),
        b_rs=dma((max(1, len(Z_UNITS)), 2)),
        c_ss=dma((max(1, len(Z_UNITS)), 2)),
        c_rs=dma((max(1, len(Z_UNITS)), 2)),
        d_ss=dma((max(1, len(Z_UNITS)),)),
        d_rs=dma((max(1, len(Z_UNITS)),)),
        z_sum=pltpu.VMEM((NZ, part, half), f32),
        z_own=pltpu.VMEM((UNITS, part, half), f32),
        z_send=pltpu.VMEM((UNITS, NZ - 1, part, half), bf16),
        z_recv=pltpu.VMEM((UNITS, NZ - 1, part, half), bf16),
        t_send=pltpu.VMEM((UNITS, part, half), f32),
        grad=pltpu.VMEM((2, 4, part, half), f32),
        kv=pltpu.VMEM((2, 2, 2, slots, head), bf16),
        state=pltpu.VMEM((3, rows, columns), f32),
        rollout=pltpu.VMEM((rows, columns), bf16),
        q_in=pltpu.VMEM((4, 2, 16 * head), bf16),
        x_in=pltpu.VMEM((4, 2, 64 * rows), bf16),
        x_mine=pltpu.VMEM((2, 32, 8, rows), f32),
        x_pair=pltpu.VMEM((32, 8, rows), f32),
        xz_send=pltpu.VMEM((NZ - 1, NX, 16, rows), bf16),
        xz_recv=pltpu.VMEM((NZ - 1, NX, 16, rows), bf16),
        xx_send=pltpu.VMEM((NX - 1, NZ, 16, rows), bf16),
        xx_recv=pltpu.VMEM((NX - 1, NZ, 16, rows), bf16),
        xx_own=pltpu.VMEM((NZ, 16, rows), bf16),
        x_all=pltpu.VMEM((NX, NZ, 16, rows), bf16),
        y_part=pltpu.VMEM((2, NX, NZ, 2, 8, half), f32),
        y_core=pltpu.VMEM((2, NX, NZ, 8, half), f32),
        yx_send=pltpu.VMEM((2, NX - 1, NZ, 8, half), f32),
        yx_recv=pltpu.VMEM((2, NX - 1, NZ, 8, half), f32),
        y_sum=pltpu.VMEM((2, NZ, 8, half), f32),
        yz_recv=pltpu.VMEM((2, NZ - 1, 8, half), f32),
        scores=pltpu.VMEM((32, slots), f32),
        query=pltpu.VMEM((2, 8, 8, head), f32),
        answer=pltpu.VMEM((2, 8, 8, head), f32),
        att=pltpu.VMEM((2, 64, head), f32),
        top=pltpu.VMEM((2, 64, head), f32),
        total=pltpu.VMEM((2, 64, head), f32),
        load_sem=dma((9,)),
        out_sem=dma((2, 4)),
        cot_ss=dma((6,)),
        cot_rs=dma((UNITS,)),
        core_ss=dma((UNITS,)),
        core_rs=dma((UNITS,)),
        x1_ss=dma((UNITS, 2)),
        x1_rs=dma((UNITS, 2)),
        x2_ss=dma((UNITS, 2)),
        x2_rs=dma((UNITS, 2)),
        z_ss=dma((UNITS,)),
        z_rs=dma((UNITS,)),
        t_ss=dma((UNITS,)),
        t_rs=dma((2, 4)),
        xc_sem=dma((2,)),
        xz_sem=dma((2,)),
        xx_ss=dma((3,)),
        xx_rs=dma((3,)),
        yc_ss=dma((2, 4)),
        yc_rs=dma((2, 4)),
        yx_ss=dma((2, 3)),
        yx_rs=dma((2, 3)),
        yz_sem=dma((2, 2)),
    )


def kernel(names, *refs):
    (lengths, q_hbm, x_hbm, f_hbm, c_hbm, w_hbm, m_hbm, v_hbm, kv_hbm) = refs[:9]
    (grad_out, new_out, att_out) = refs[9:12]
    r = types.SimpleNamespace(**dict(zip(names, refs[12:])))
    x, y, z, core = position()
    other = 1 - core
    flip, mirror = x + 1 - 2 * (x % 2), 3 - x
    first_partner, second_partner = (flip, mirror), (mirror, flip)
    rows, columns = r.rollout.shape
    part, half = rows // 4, columns // 2
    tokens = r.feat.shape[0]
    slots, head = r.kv.shape[3:]
    scale = head**-0.5

    loads = [
        pltpu.make_async_copy(source, target, r.load_sem.at[i])
        for i, (source, target) in enumerate(
            (
                (c_hbm.at[:, pl.ds(0, half)], r.cot.at[0]),
                (f_hbm, r.feat),
                (c_hbm.at[:, pl.ds(half, half)], r.cot.at[1]),
                (kv_hbm, r.kv),
                (w_hbm, r.state.at[0]),
                (m_hbm, r.state.at[1]),
                (v_hbm, r.state.at[2]),
                (q_hbm, r.q_in),
                (x_hbm, r.x_in),
            )
        )
    ]
    for index in (1, 0, 2, 8):
        loads[index].start()

    barrier = pltpu.get_barrier_semaphore()

    def greet(where):
        pl.semaphore_signal(barrier, inc=1, device_id=where, device_id_type=MESH)

    greet(device(x, y, z, other))
    for k in range(1, NX):
        greet(device((x + k) % NX, y, z, core))
    for k in range(1, NZ):
        greet(device(x, y, (z + k) % NZ, core))
    for k in range(1, NY):
        greet(device(x, (y + k) % NY, z, core))
    for k in range(4):

        @pl.when(jnp.logical_or(x != y, y != k))
        def _():
            greet(device(y, k, z, core))

        @pl.when(jnp.logical_or(x != y, x != k))
        def _():
            greet(device(k, x, z, core))

    same = (4 - (x - y + 4) % 4) // 4
    pl.semaphore_wait(barrier, 1 + (NX - 1) + (NZ - 1) + (NY - 1) + 8 - 2 * same)

    slot = {place: unit for unit, place in enumerate(PLACES)}
    arrived = {slot[0, 0]}

    def cot_copy(index):
        step = (3, 1, 3, 1, 1, 3)[index]
        half_of = (0, 0, 1, 1, 0, 1)[index]
        source = slot[0, half_of] if index < 4 else slot[(3, 1)[half_of], half_of]
        target = slot[4 - step, half_of] if index < 4 else slot[2, half_of]
        start = c_hbm.at[:, pl.ds(half_of * half, half)] if index < 4 else r.cot.at[source]
        return send(
            start,
            r.cot.at[target],
            r.cot_ss.at[index],
            r.cot_rs.at[target],
            device(x, (y + step) % NY, z, core),
        )

    def have(unit):
        if unit == slot[0, 1] and unit not in arrived:
            loads[2].wait()
        elif unit not in arrived:
            send(
                r.cot.at[unit],
                r.cot.at[unit],
                r.cot_ss.at[0],
                r.cot_rs.at[unit],
                device(x, (y + 1) % NY, z, core),
            ).wait_recv()
        arrived.add(unit)

    def forward(part_of):
        have(slot[(3, 1)[part_of], part_of])
        cot_copy(4 + part_of).start()

    x_swap = send(
        r.x_mine.at[other],
        r.x_pair,
        r.xc_sem.at[0],
        r.xc_sem.at[1],
        device(x, y, z, other),
    )
    for index in range(4):
        cot_copy(index).start()
    loads[8].wait()
    inputs = jnp.concatenate([r.x_in[s].astype(f32) for s in range(4)], axis=0)
    for block in range(64):
        r.x_mine[block % 2, block // 2] = inputs[:, block * rows : (block + 1) * rows]
    x_swap.start()
    loads[0].wait()
    loads[1].wait()
    for index in range(3, 8):
        loads[index].start()

    def turn(side):
        for row_block in range(NZ):
            columns_of = pl.ds(pl.multiple_of((row_block * 2 + side) * rows, rows), rows)
            r.turned[side, row_block] = r.feat[:, columns_of].T

    def multiply(side, unit, store):
        def step(i, carry):
            left = r.turned[side, pl.ds(2 * i, 2)].reshape(2 * rows, tokens)
            product = jnp.dot(left, r.cot[unit], preferred_element_type=f32)
            store(i, product.reshape(2, 4, part, half))
            return carry

        lax.fori_loop(0, NZ // 2, step, 0)

    def core_copy(unit):
        return send(
            r.core_send.at[unit],
            r.core_recv.at[unit],
            r.core_ss.at[unit],
            r.core_rs.at[unit],
            device(x, y, z, other),
        )

    def x1_copy(unit, side):
        return send(
            r.x1_send.at[unit, side],
            r.x1_recv.at[unit, side],
            r.x1_ss.at[unit, side],
            r.x1_rs.at[unit, side],
            device(first_partner[side], y, z, core),
        )

    def x2_copy(unit, side):
        return send(
            r.x2_send.at[unit, side],
            r.x2_recv.at[unit, side],
            r.x2_ss.at[unit, side],
            r.x2_rs.at[unit, side],
            device(second_partner[side], y, z, core),
        )

    def z_copy(unit, k):
        return send(
            r.z_send.at[unit, k - 1],
            r.z_recv.at[unit, k - 1],
            r.z_ss.at[unit],
            r.z_rs.at[unit],
            device(x, y, (z + k) % NZ, core),
        )

    def z_all(unit):
        return send(
            r.z_send.at[unit],
            r.z_recv.at[unit],
            r.z_ss.at[unit],
            r.z_rs.at[unit],
            device(x, y, (z + 1) % NZ, core),
        )

    def t_copy(unit):
        away, which = PLACES[unit]
        return send(
            r.t_send.at[unit],
            r.grad.at[which, x],
            r.t_ss.at[unit],
            r.t_rs.at[which, x],
            device(y, (y + away) % NY, z, core),
        )

    def stage0(unit):
        have(unit)

        def store(i, product):
            r.core_send[unit, pl.ds(2 * i, 2)] = product.astype(bf16)

        multiply(other, unit, store)
        core_copy(unit).start()

    def own(unit):
        if unit == 0:
            turn(core)

        def store(i, product):
            r.mine[pl.ds(2 * i, 2)] = product

        multiply(core, unit, store)

    def stage1(unit):
        core_copy(unit).wait()
        if unit in Z_UNITS:
            at_unit = Z_UNITS.index(unit)
            for side in range(2):
                for at in range(2):
                    block = 2 * (2 * side + at) + 1 - z % 2
                    r.a_send[at_unit, side, at] = (
                        r.mine[block] + r.core_recv[unit, block].astype(f32)
                    ).astype(bf16)
                a_copy(unit, side).start()
            for side in range(2):
                for at in range(2):
                    block = 2 * (2 * side + at) + z % 2
                    r.a_keep[at_unit, side, at] = r.mine[block] + r.core_recv[
                        unit, block
                    ].astype(f32)

        else:
            for side in range(2):
                partner = first_partner[side]
                away = (partner, (3 - partner, partner + 1 - 2 * (partner % 2))[side])
                for k in range(2):
                    for at in range(4):
                        row_block = side * 4 + at
                        r.x1_send[unit, side, k, at] = (
                            r.mine[row_block, away[k]]
                            + r.core_recv[unit, row_block, away[k]].astype(f32)
                        ).astype(bf16)
                x1_copy(unit, side).start()
            for side in range(2):
                near = (x, second_partner[side])
                for k in range(2):
                    for at in range(4):
                        row_block = side * 4 + at
                        r.keep[unit, side, k, at] = r.mine[row_block, near[k]] + r.core_recv[
                            unit, row_block, near[k]
                        ].astype(f32)

    def a_copy(unit, side):
        return send(
            r.a_send.at[Z_UNITS.index(unit), side],
            r.a_recv.at[Z_UNITS.index(unit), side],
            r.a_ss.at[Z_UNITS.index(unit), side],
            r.a_rs.at[Z_UNITS.index(unit), side],
            device(x, y, (z + 1 - 2 * (z % 2), (z + 7 + 2 * (z % 2)) % NZ)[side], core),
        )

    def b_copy(unit, side):
        return send(
            r.b_send.at[Z_UNITS.index(unit), side],
            r.b_recv.at[Z_UNITS.index(unit), side],
            r.b_ss.at[Z_UNITS.index(unit), side],
            r.b_rs.at[Z_UNITS.index(unit), side],
            device(first_partner[side], y, z, core),
        )

    def c_copy(unit, side):
        return send(
            r.c_send.at[Z_UNITS.index(unit), side],
            r.c_recv.at[Z_UNITS.index(unit), side],
            r.c_ss.at[Z_UNITS.index(unit), side],
            r.c_rs.at[Z_UNITS.index(unit), side],
            device(second_partner[side], y, z, core),
        )

    def d_copy(unit, k):
        return send(
            r.d_send.at[Z_UNITS.index(unit), k - 1],
            r.d_recv.at[Z_UNITS.index(unit), k - 1],
            r.d_ss.at[Z_UNITS.index(unit)],
            r.d_rs.at[Z_UNITS.index(unit)],
            device(x, y, (z + 2 * k) % NZ, core),
        )

    def d_all(unit):
        return send(
            r.d_send.at[Z_UNITS.index(unit)],
            r.d_recv.at[Z_UNITS.index(unit)],
            r.d_ss.at[Z_UNITS.index(unit)],
            r.d_rs.at[Z_UNITS.index(unit)],
            device(x, y, (z + 2) % NZ, core),
        )

    def away_and_near(side):
        partner = first_partner[side]
        away = (partner, (3 - partner, partner + 1 - 2 * (partner % 2))[side])
        return away, (x, second_partner[side])

    def z_stage2(unit):
        at_unit = Z_UNITS.index(unit)
        for side in range(2):
            a_copy(unit, side).wait()
            away, near = away_and_near(side)
            for k in range(2):
                for at in range(2):
                    r.b_send[at_unit, side, k, at] = (
                        r.a_keep[at_unit, side, at, away[k]]
                        + r.a_recv[at_unit, side, at, away[k]].astype(f32)
                    ).astype(bf16)
            b_copy(unit, side).start()
            for k in range(2):
                for at in range(2):
                    r.b_keep[at_unit, side, k, at] = r.a_keep[
                        at_unit, side, at, near[k]
                    ] + r.a_recv[at_unit, side, at, near[k]].astype(f32)

    def z_stage3(unit):
        at_unit = Z_UNITS.index(unit)
        for side in range(2):
            b_copy(unit, side).wait()
            r.c_send[at_unit, side] = (
                r.b_keep[at_unit, side, 1] + r.b_recv[at_unit, side, 1].astype(f32)
            ).astype(bf16)
            c_copy(unit, side).start()
            r.b_keep[at_unit, side, 0] += r.b_recv[at_unit, side, 0].astype(f32)

    def z_stage4(unit):
        at_unit = Z_UNITS.index(unit)
        for side in range(2):
            c_copy(unit, side).wait()
            for at in range(2):
                r.d_sum[side * 2 + at] = r.b_keep[at_unit, side, 0, at] + r.c_recv[
                    at_unit, side, at
                ].astype(f32)
        for k in (2, 1, 3):
            r.d_send[at_unit, k - 1] = r.d_sum[(z // 2 + k) % 4].astype(bf16)
            d_copy(unit, k).start()
        r.z_own[unit] = r.d_sum[z // 2]

    def z_stage5(unit):
        d_all(unit).wait()
        total = r.z_own[unit]
        for k in range(3):
            total = total + r.d_recv[Z_UNITS.index(unit), k].astype(f32)
        finish(unit, total)

    def stage2(unit):
        for side in range(2):
            x1_copy(unit, side).wait()
            r.x2_send[unit, side] = (
                r.keep[unit, side, 1] + r.x1_recv[unit, side, 1].astype(f32)
            ).astype(bf16)
            x2_copy(unit, side).start()
        for side in range(2):
            r.keep[unit, side, 0] += r.x1_recv[unit, side, 0].astype(f32)

    def stage3(unit):
        for side in range(2):
            x2_copy(unit, side).wait()
            for at in range(4):
                r.z_sum[side * 4 + at] = r.keep[unit, side, 0, at] + r.x2_recv[
                    unit, side, at
                ].astype(f32)
        for k in (4, 3, 5, 2, 6, 1, 7):
            r.z_send[unit, k - 1] = r.z_sum[(z + k) % NZ].astype(bf16)
            z_copy(unit, k).start()
        r.z_own[unit] = r.z_sum[z]

    def stage4(unit):
        z_all(unit).wait()
        total = r.z_own[unit]
        for k in range(NZ - 1):
            total = total + r.z_recv[unit, k].astype(f32)
        finish(unit, total)

    def finish(unit, total):
        away, which = PLACES[unit]

        def go():
            r.t_send[unit] = total
            t_copy(unit).start()

        if away == 0:

            @pl.when(x == y)
            def _():
                r.grad[which, x] = total

            pl.when(x != y)(go)
        else:
            go()

    def xx_copy(k):
        return send(
            r.xx_send.at[k - 1],
            r.xx_recv.at[k - 1],
            r.xx_ss.at[k - 1],
            r.xx_rs.at[k - 1],
            device((x + k) % NX, y, z, core),
        )

    def xz_copy(k, source, target):
        return send(
            source,
            target,
            r.xz_sem.at[0],
            r.xz_sem.at[1],
            device(x, y, (z + k) % NZ, core),
        )

    def spread_x(_):
        x_swap.wait()
        for k in (2, 1, 3, 0):
            target = r.xx_own if k == 0 else r.xx_send.at[k - 1]
            for block in range(NZ):
                at = (x + k) % NX * NZ + block
                mine, pair = r.x_mine[core, at], r.x_pair[at]
                low, high = jnp.where(core == 0, mine, pair), jnp.where(core == 0, pair, mine)
                target[block] = jnp.concatenate([low, high], axis=0).astype(bf16)
            if k > 0:
                xx_copy(k).start()

    def spread_z(_):
        for k in range(1, NX):
            xx_copy(k).wait()
        for k in (4, 3, 5, 2, 6, 1, 7):
            to = (z + k) % NZ
            r.xz_send[k - 1, 0] = r.xx_own[to]
            for j in range(1, NX):
                r.xz_send[k - 1, j] = r.xx_recv[j - 1, to]
            xz_copy(k, r.xz_send.at[k - 1], r.xz_recv.at[k - 1]).start()

    def spread_done():
        xz_copy(1, r.xz_send, r.xz_recv).wait()
        r.x_all[0, z] = r.xx_own[z]
        for j in range(1, NX):
            r.x_all[j, z] = r.xx_recv[j - 1, z]
        for k in range(1, NZ):
            for j in range(NX):
                r.x_all[j, (z + NZ - k) % NZ] = r.xz_recv[k - 1, j]
        for k in range(4, 7):
            loads[k].wait()

    chunk = min(1024, slots)

    def cached(pair):
        row, kv_head = pair // 2, pair % 2
        if pair == 0:
            loads[3].wait()
            loads[7].wait()
            asked = jnp.concatenate([r.q_in[s].astype(f32) for s in range(4)], axis=0)
            for h in range(2):
                for g in range(8):
                    r.query[h, :, g, :] = asked[:, (h * 8 + g) * head : (h * 8 + g + 1) * head]
        query = r.query[kv_head].reshape(4, 2, 8, head)
        query = query[:, row].reshape(32, head).astype(bf16)

        def score(i, highest):
            at = pl.ds(pl.multiple_of(i * chunk, chunk), chunk)
            value = lax.dot_general(
                query,
                r.kv[0, row, kv_head, at],
                (((1,), (1,)), ((), ())),
                preferred_element_type=f32,
            )
            places = i * chunk + lax.broadcasted_iota(jnp.int32, value.shape, 1)
            value = jnp.where(places < lengths[row], value * scale, -jnp.inf)
            r.scores[:, at] = value
            return jnp.maximum(highest, jnp.max(value, axis=1, keepdims=True))

        highest = lax.fori_loop(0, slots // chunk, score, jnp.full((32, 1), -jnp.inf, f32))

        def weigh(i, carry):
            total, result = carry
            at = pl.ds(pl.multiple_of(i * chunk, chunk), chunk)
            weight = jnp.exp(r.scores[:, at] - highest)
            total = total + jnp.sum(weight, axis=1, keepdims=True)
            result = result + jnp.dot(
                weight.astype(bf16), r.kv[1, row, kv_head, at], preferred_element_type=f32
            )
            return total, result

        total, result = lax.fori_loop(
            0, slots // chunk, weigh, (jnp.zeros((32, 1), f32), jnp.zeros((32, head), f32))
        )
        highest = jnp.broadcast_to(highest, (32, head))
        total = jnp.broadcast_to(total, (32, head))
        for s in range(4):
            at = pl.ds(s * 16 + row * 8, 8)
            one = slice(s * 8, s * 8 + 8)
            r.att[kv_head, at] = result[one]
            r.top[kv_head, at] = highest[one]
            r.total[kv_head, at] = total[one]

    def store_copy(which, s):
        return pltpu.make_async_copy(
            r.grad.at[which, s],
            grad_out.at[pl.ds(s * part, part), pl.ds(which * half, half)],
            r.out_sem.at[which, s],
        )

    def yc_copy(which, k):
        return send(
            r.y_part.at[which, k, :, other],
            r.y_core.at[which, k],
            r.yc_ss.at[which, k],
            r.yc_rs.at[which, k],
            device(x, y, z, other),
        )

    def yx_copy(which, k):
        return send(
            r.yx_send.at[which, k - 1],
            r.yx_recv.at[which, k - 1],
            r.yx_ss.at[which, k - 1],
            r.yx_rs.at[which, k - 1],
            device((x + NX - k) % NX, y, z, core),
        )

    def yz_copy(which, k):
        return send(
            r.y_sum.at[which, (z + k) % NZ],
            r.yz_recv.at[which, k - 1],
            r.yz_sem.at[which, 0],
            r.yz_sem.at[which, 1],
            device(x, y, (z + k) % NZ, core),
        )

    def new0(which):
        if which == first_head:
            spread_done()
        for s in range(4):

            @pl.when(jnp.logical_or(x != y, x != s))
            def _():
                send(
                    r.t_send.at[0],
                    r.grad.at[which, s],
                    r.t_ss.at[0],
                    r.t_rs.at[which, s],
                    device(x, (y + 1) % NY, z, core),
                ).wait_recv()

            at = (pl.ds(s * part, part), pl.ds(which * half, half))
            master, _, _ = adam(r.grad[which, s], *(r.state[i, at[0], at[1]] for i in range(3)))
            r.rollout[at[0], at[1]] = master.astype(bf16)
        for k in (2, 1, 3, 0):
            product = jnp.dot(
                r.x_all[k].reshape(NZ * 16, rows),
                r.rollout[:, which * half : (which + 1) * half],
                preferred_element_type=f32,
            )
            r.y_part[which, k] = product.reshape(NZ, 2, 8, half)
            yc_copy(which, k).start()
        for s in range(4):
            store_copy(which, s).start()

    def new1(which):
        for k in (2, 1, 3):
            yc_copy(which, k).wait()
            r.yx_send[which, k - 1] = r.y_part[which, k, :, core] + r.y_core[which, k]
            yx_copy(which, k).start()
        yc_copy(which, 0).wait()
        r.y_sum[which] = r.y_part[which, 0, :, core] + r.y_core[which, 0]

    def new2(which):
        for k in (1, 3, 2):
            yx_copy(which, k).wait()
            r.y_sum[which] += r.yx_recv[which, k - 1]
        for k in (4, 3, 5, 2, 6, 1, 7):
            yz_copy(which, k).start()

    def new3(which):
        send(
            r.y_sum.at[which, pl.ds(0, NZ - 1)],
            r.yz_recv.at[which],
            r.yz_sem.at[which, 0],
            r.yz_sem.at[which, 1],
            device(x, y, (z + 1) % NZ, core),
        ).wait()
        fresh = r.y_sum[which, z]
        for k in range(NZ - 1):
            fresh = fresh + r.yz_recv[which, k]
        for s in range(4):
            new_out[s, :, pl.ds(which * half, half)] = fresh[2 * s : 2 * s + 2].astype(bf16)
        fresh = fresh.astype(bf16)
        key, value = fresh[:, :head], fresh[:, head:]
        line = lax.broadcasted_iota(jnp.int32, (64, 8), 0)
        spot = lax.broadcasted_iota(jnp.int32, (64, 8), 1)
        allowed = jnp.logical_and((line // 8) % 2 == spot % 2, spot // 2 <= line // 16)
        score = lax.dot_general(
            r.query[which].reshape(64, head).astype(bf16),
            key,
            (((1,), (1,)), ((), ())),
            preferred_element_type=f32,
        )
        score = jnp.where(allowed, score * scale, -jnp.inf)
        before = r.top[which][:, :1]
        highest = jnp.maximum(before, jnp.max(score, axis=1, keepdims=True))
        weight = jnp.exp(score - highest)
        factor = jnp.exp(before - highest)
        total = r.total[which][:, :1] * factor + jnp.sum(weight, axis=1, keepdims=True)
        result = r.att[which] * factor + jnp.dot(
            weight.astype(bf16), value, preferred_element_type=f32
        )
        r.answer[which] = (result / total).reshape(8, 8, head)
        for g in range(8):
            value = r.answer[which, :, g, :]
            at = pl.ds((which * 8 + g) * head, head)
            for s in range(4):
                att_out[s, :, at] = value[2 * s : 2 * s + 2].astype(bf16)

    steps = dict(
        F=forward,
        X=spread_x,
        Y=spread_z,
        A=cached,
        B=stage0,
        C=own,
        D=stage1,
        E=stage2,
        G=stage3,
        H=stage4,
        I=z_stage2,
        J=z_stage3,
        K=z_stage4,
        L=z_stage5,
        P=new0,
        Q=new1,
        R=new2,
        S=new3,
    )
    order = [(word[0], int(word[1])) for word in ORDER]
    first_head = [place for name, place in order if name == NEW][0]
    turn(other)
    for name, place in order:
        steps[name](place)
    for unit in range(UNITS):
        if PLACES[unit][0] == 0:
            pl.when(x != y)(lambda: t_copy(unit).wait_send())
        else:
            t_copy(unit).wait_send()
    for index in range(6):
        cot_copy(index).wait_send()
    for which in range(2):
        for s in range(4):
            store_copy(which, s).wait()


def last(gradient, master, first, second, new_kv, attended, *results):
    values = (*adam(gradient[...], master[...], first[...], second[...]), new_kv[...], attended[...])
    for result, value in zip(results, values):
        result[...] = value


def shards(
    features,
    kv_cotangent,
    master_weight,
    first_moment,
    second_moment,
    decode_inputs,
    queries,
    kv_cache,
    cache_lengths,
):
    tokens = features.shape[0]
    rows, columns = master_weight.shape
    steps, own_rows, width = decode_inputs.shape
    heads, slots, head = kv_cache.shape[2:]
    shapes = scratch(rows, columns, tokens, slots, head)
    in_vmem = pl.BlockSpec(memory_space=pltpu.VMEM)
    anywhere = pl.BlockSpec(memory_space=pl.ANY)
    gradient, new_kv, attended = pl.pallas_call(
        functools.partial(kernel, tuple(shapes)),
        out_shape=(
            jax.ShapeDtypeStruct((rows, columns), f32),
            jax.ShapeDtypeStruct((steps, own_rows, columns), bf16),
            jax.ShapeDtypeStruct(queries.shape, bf16),
        ),
        in_specs=[pl.BlockSpec(memory_space=pltpu.SMEM)] + [anywhere] * 8,
        out_specs=(anywhere, in_vmem, in_vmem),
        scratch_shapes=list(shapes.values()),
        compiler_params=pltpu.CompilerParams(
            collective_id=0, has_side_effects=True, vmem_limit_bytes=56 * 2**20
        ),
        name="fused_step",
    )(
        cache_lengths,
        queries,
        decode_inputs,
        features,
        kv_cotangent,
        master_weight,
        first_moment,
        second_moment,
        kv_cache,
    )
    like = jax.ShapeDtypeStruct((rows, columns), f32)
    return pl.pallas_call(
        last,
        out_shape=(
            like,
            like,
            like,
            jax.ShapeDtypeStruct(new_kv.shape, bf16),
            jax.ShapeDtypeStruct(attended.shape, bf16),
        ),
        in_specs=[in_vmem] * 6,
        out_specs=[in_vmem] * 5,
        name="last",
    )(gradient, master_weight, first_moment, second_moment, new_kv, attended)


def solution(mesh):
    in_specs = (
        P(("learn", "dp"), "tp"),
        P(("learn", "dp"), "tp"),
        P(("learn", "dp"), "tp"),
        P(("learn", "dp"), "tp"),
        P(("learn", "dp"), "tp"),
        P(None, ("learn", "dp"), None),
        P(None, ("learn", "dp"), "tp"),
        P(None, ("learn", "dp"), "tp", None, None),
        P(("learn", "dp")),
    )
    out_specs = (
        P(("learn", "dp"), "tp"),
        P(("learn", "dp"), "tp"),
        P(("learn", "dp"), "tp"),
        P(None, ("learn", "dp"), "tp"),
        P(None, ("learn", "dp"), "tp"),
    )
    return jax.shard_map(shards, mesh=mesh, in_specs=in_specs, out_specs=out_specs, check_vma=False)
```

```python
import functools
import types

import jax
import jax.numpy as jnp
from jax import lax
from jax.experimental import pallas as pl
from jax.experimental.pallas import tpu as pltpu
from jax.sharding import PartitionSpec as P

learn_rate = 0.005
decay_rate = 0.1
first_fix = 1.0 - 0.9**10
second_fix = 1.0 - 0.999**10

MESH = pl.DeviceIdType.MESH
UNITS = 8
NX, NY, NZ = 4, 4, 8
NEW = 'P'
PLACES = ((0, 0), (0, 1), (1, 0), (3, 0), (1, 1), (3, 1), (2, 0), (2, 1))
Z_UNITS = (1, 2, 4, 6, 7)
ORDER = (
    "B0", "B1", "X0", "C0", "D0", "C1", "D1", "Y0", "A0", "F0", "B2", "B3",
    "E0", "C2", "A1", "I1", "D2", "C3", "F1", "G0", "B4", "B5", "D3", "C4",
    "J1", "A2", "I2", "D4", "B6", "C5", "D5", "C6", "E3", "K1", "B7", "H0",
    "D6", "J2", "C7", "I4", "A3", "D7", "E5", "L1", "G3", "K2", "I6", "J4",
    "I7", "G5", "J6", "K4", "J7", "H3", "K6", "L2", "K7", "H5", "L4", "L6",
    "L7", "P0", "P1", "Q0", "Q1", "R0", "R1", "S0", "S1",
)

bf16 = jnp.bfloat16
f32 = jnp.float32


def position():
    learn, dp = lax.axis_index("learn"), lax.axis_index("dp")
    return learn // 4, lax.axis_index("tp"), (learn % 4) * 2 + dp // 2, dp % 2


def device(x, y, z, core):
    return {"learn": x * 4 + z // 2, "tp": y, "dp": (z % 2) * 2 + core}


def send(source, target, send_sem, recv_sem, where):
    return pltpu.make_async_remote_copy(
        src_ref=source,
        dst_ref=target,
        send_sem=send_sem,
        recv_sem=recv_sem,
        device_id=where,
        device_id_type=MESH,
    )


def adam(gradient, master, first, second):
    first = 0.9 * first + 0.1 * gradient
    second = 0.999 * second + 0.001 * gradient * gradient
    update = (first / first_fix) / (jnp.sqrt(second / second_fix) + 1e-08)
    return master - learn_rate * (update + decay_rate * master), first, second


def scratch(rows, columns, tokens, slots, head):
    part, half = rows // 4, columns // 2
    dma = pltpu.SemaphoreType.DMA
    return dict(
        feat=pltpu.VMEM((tokens, 16 * rows), bf16),
        turned=pltpu.VMEM((2, NZ, rows, tokens), bf16),
        cot=pltpu.VMEM((UNITS, tokens, half), bf16),
        core_send=pltpu.VMEM((UNITS, NZ, 4, part, half), bf16),
        core_recv=pltpu.VMEM((UNITS, NZ, 4, part, half), bf16),
        mine=pltpu.VMEM((NZ, 4, part, half), f32),
        keep=pltpu.VMEM((UNITS, 2, 2, 4, part, half), f32),
        x1_send=pltpu.VMEM((UNITS, 2, 2, 4, part, half), bf16),
        x1_recv=pltpu.VMEM((UNITS, 2, 2, 4, part, half), bf16),
        x2_send=pltpu.VMEM((UNITS, 2, 4, part, half), bf16),
        x2_recv=pltpu.VMEM((UNITS, 2, 4, part, half), bf16),
        a_send=pltpu.VMEM((max(1, len(Z_UNITS)), 2, 2, 4, part, half), bf16),
        a_recv=pltpu.VMEM((max(1, len(Z_UNITS)), 2, 2, 4, part, half), bf16),
        a_keep=pltpu.VMEM((max(1, len(Z_UNITS)), 2, 2, 4, part, half), f32),
        b_keep=pltpu.VMEM((max(1, len(Z_UNITS)), 2, 2, 2, part, half), f32),
        b_send=pltpu.VMEM((max(1, len(Z_UNITS)), 2, 2, 2, part, half), bf16),
        b_recv=pltpu.VMEM((max(1, len(Z_UNITS)), 2, 2, 2, part, half), bf16),
        c_send=pltpu.VMEM((max(1, len(Z_UNITS)), 2, 2, part, half), bf16),
        c_recv=pltpu.VMEM((max(1, len(Z_UNITS)), 2, 2, part, half), bf16),
        d_sum=pltpu.VMEM((4, part, half), f32),
        d_send=pltpu.VMEM((max(1, len(Z_UNITS)), 3, part, half), bf16),
        d_recv=pltpu.VMEM((max(1, len(Z_UNITS)), 3, part, half), bf16),
        a_ss=dma((max(1, len(Z_UNITS)), 2)),
        a_rs=dma((max(1, len(Z_UNITS)), 2)),
        b_ss=dma((max(1, len(Z_UNITS)), 2)),
        b_rs=dma((max(1, len(Z_UNITS)), 2)),
        c_ss=dma((max(1, len(Z_UNITS)), 2)),
        c_rs=dma((max(1, len(Z_UNITS)), 2)),
        d_ss=dma((max(1, len(Z_UNITS)),)),
        d_rs=dma((max(1, len(Z_UNITS)),)),
        z_sum=pltpu.VMEM((NZ, part, half), f32),
        z_own=pltpu.VMEM((UNITS, part, half), f32),
        z_send=pltpu.VMEM((UNITS, NZ - 1, part, half), bf16),
        z_recv=pltpu.VMEM((UNITS, NZ - 1, part, half), bf16),
        t_send=pltpu.VMEM((UNITS, part, half), f32),
        grad=pltpu.VMEM((2, 4, part, half), f32),
        kv=pltpu.VMEM((2, 2, 2, slots, head), bf16),
        state=pltpu.VMEM((3, rows, columns), f32),
        rollout=pltpu.VMEM((rows, columns), bf16),
        q_in=pltpu.VMEM((4, 2, 16 * head), bf16),
        x_in=pltpu.VMEM((4, 2, 64 * rows), bf16),
        x_mine=pltpu.VMEM((2, 32, 8, rows), f32),
        x_pair=pltpu.VMEM((32, 8, rows), f32),
        xz_send=pltpu.VMEM((NZ - 1, NX, 16, rows), bf16),
        xz_recv=pltpu.VMEM((NZ - 1, NX, 16, rows), bf16),
        xx_send=pltpu.VMEM((NX - 1, NZ, 16, rows), bf16),
        xx_recv=pltpu.VMEM((NX - 1, NZ, 16, rows), bf16),
        xx_own=pltpu.VMEM((NZ, 16, rows), bf16),
        x_all=pltpu.VMEM((NX, NZ, 16, rows), bf16),
        y_part=pltpu.VMEM((2, NX, NZ, 2, 8, half), f32),
        y_core=pltpu.VMEM((2, NX, NZ, 8, half), f32),
        yx_send=pltpu.VMEM((2, NX - 1, NZ, 8, half), f32),
        yx_recv=pltpu.VMEM((2, NX - 1, NZ, 8, half), f32),
        y_sum=pltpu.VMEM((2, NZ, 8, half), f32),
        yz_recv=pltpu.VMEM((2, NZ - 1, 8, half), f32),
        scores=pltpu.VMEM((32, slots), f32),
        query=pltpu.VMEM((2, 8, 8, head), f32),
        answer=pltpu.VMEM((2, 8, 8, head), f32),
        att=pltpu.VMEM((2, 64, head), f32),
        top=pltpu.VMEM((2, 64, head), f32),
        total=pltpu.VMEM((2, 64, head), f32),
        load_sem=dma((9,)),
        out_sem=dma((2, 4)),
        cot_ss=dma((6,)),
        cot_rs=dma((UNITS,)),
        core_ss=dma((UNITS,)),
        core_rs=dma((UNITS,)),
        x1_ss=dma((UNITS, 2)),
        x1_rs=dma((UNITS, 2)),
        x2_ss=dma((UNITS, 2)),
        x2_rs=dma((UNITS, 2)),
        z_ss=dma((UNITS,)),
        z_rs=dma((UNITS,)),
        t_ss=dma((UNITS,)),
        t_rs=dma((2, 4)),
        xc_sem=dma((2,)),
        xz_sem=dma((2,)),
        xx_ss=dma((3,)),
        xx_rs=dma((3,)),
        yc_ss=dma((2, 4)),
        yc_rs=dma((2, 4)),
        yx_ss=dma((2, 3)),
        yx_rs=dma((2, 3)),
        yz_sem=dma((2, 2)),
    )


def kernel(names, *refs):
    (lengths, q_hbm, x_hbm, f_hbm, c_hbm, w_hbm, m_hbm, v_hbm, kv_hbm) = refs[:9]
    (grad_out, new_out, att_out) = refs[9:12]
    r = types.SimpleNamespace(**dict(zip(names, refs[12:])))
    x, y, z, core = position()
    other = 1 - core
    flip, mirror = x + 1 - 2 * (x % 2), 3 - x
    first_partner, second_partner = (flip, mirror), (mirror, flip)
    rows, columns = r.rollout.shape
    part, half = rows // 4, columns // 2
    tokens = r.feat.shape[0]
    slots, head = r.kv.shape[3:]
    scale = head**-0.5

    loads = [
        pltpu.make_async_copy(source, target, r.load_sem.at[i])
        for i, (source, target) in enumerate(
            (
                (c_hbm.at[:, pl.ds(0, half)], r.cot.at[0]),
                (f_hbm, r.feat),
                (c_hbm.at[:, pl.ds(half, half)], r.cot.at[1]),
                (kv_hbm, r.kv),
                (w_hbm, r.state.at[0]),
                (m_hbm, r.state.at[1]),
                (v_hbm, r.state.at[2]),
                (q_hbm, r.q_in),
                (x_hbm, r.x_in),
            )
        )
    ]
    for index in (1, 0, 2, 8):
        loads[index].start()

    barrier = pltpu.get_barrier_semaphore()

    def greet(where):
        pl.semaphore_signal(barrier, inc=1, device_id=where, device_id_type=MESH)

    greet(device(x, y, z, other))
    for k in range(1, NX):
        greet(device((x + k) % NX, y, z, core))
    for k in range(1, NZ):
        greet(device(x, y, (z + k) % NZ, core))
    for k in range(1, NY):
        greet(device(x, (y + k) % NY, z, core))
    for k in range(4):

        @pl.when(jnp.logical_or(x != y, y != k))
        def _():
            greet(device(y, k, z, core))

        @pl.when(jnp.logical_or(x != y, x != k))
        def _():
            greet(device(k, x, z, core))

    same = (4 - (x - y + 4) % 4) // 4
    pl.semaphore_wait(barrier, 1 + (NX - 1) + (NZ - 1) + (NY - 1) + 8 - 2 * same)

    slot = {place: unit for unit, place in enumerate(PLACES)}
    arrived = {slot[0, 0]}

    def cot_copy(index):
        step = (3, 1, 3, 1, 1, 3)[index]
        half_of = (0, 0, 1, 1, 0, 1)[index]
        source = slot[0, half_of] if index < 4 else slot[(3, 1)[half_of], half_of]
        target = slot[4 - step, half_of] if index < 4 else slot[2, half_of]
        start = c_hbm.at[:, pl.ds(half_of * half, half)] if index < 4 else r.cot.at[source]
        return send(
            start,
            r.cot.at[target],
            r.cot_ss.at[index],
            r.cot_rs.at[target],
            device(x, (y + step) % NY, z, core),
        )

    def have(unit):
        if unit == slot[0, 1] and unit not in arrived:
            loads[2].wait()
        elif unit not in arrived:
            send(
                r.cot.at[unit],
                r.cot.at[unit],
                r.cot_ss.at[0],
                r.cot_rs.at[unit],
                device(x, (y + 1) % NY, z, core),
            ).wait_recv()
        arrived.add(unit)

    def forward(part_of):
        have(slot[(3, 1)[part_of], part_of])
        cot_copy(4 + part_of).start()

    x_swap = send(
        r.x_mine.at[other],
        r.x_pair,
        r.xc_sem.at[0],
        r.xc_sem.at[1],
        device(x, y, z, other),
    )
    for index in range(4):
        cot_copy(index).start()
    loads[8].wait()
    inputs = jnp.concatenate([r.x_in[s].astype(f32) for s in range(4)], axis=0)
    for block in range(64):
        r.x_mine[block % 2, block // 2] = inputs[:, block * rows : (block + 1) * rows]
    x_swap.start()
    loads[0].wait()
    loads[1].wait()
    for index in range(3, 8):
        loads[index].start()

    def turn(side):
        for row_block in range(NZ):
            columns_of = pl.ds(pl.multiple_of((row_block * 2 + side) * rows, rows), rows)
            r.turned[side, row_block] = r.feat[:, columns_of].T

    def multiply(side, unit, store):
        def step(i, carry):
            left = r.turned[side, pl.ds(2 * i, 2)].reshape(2 * rows, tokens)
            product = jnp.dot(left, r.cot[unit], preferred_element_type=f32)
            store(i, product.reshape(2, 4, part, half))
            return carry

        lax.fori_loop(0, NZ // 2, step, 0, unroll=True)

    def core_copy(unit):
        return send(
            r.core_send.at[unit],
            r.core_recv.at[unit],
            r.core_ss.at[unit],
            r.core_rs.at[unit],
            device(x, y, z, other),
        )

    def x1_copy(unit, side):
        return send(
            r.x1_send.at[unit, side],
            r.x1_recv.at[unit, side],
            r.x1_ss.at[unit, side],
            r.x1_rs.at[unit, side],
            device(first_partner[side], y, z, core),
        )

    def x2_copy(unit, side):
        return send(
            r.x2_send.at[unit, side],
            r.x2_recv.at[unit, side],
            r.x2_ss.at[unit, side],
            r.x2_rs.at[unit, side],
            device(second_partner[side], y, z, core),
        )

    def z_copy(unit, k):
        return send(
            r.z_send.at[unit, k - 1],
            r.z_recv.at[unit, k - 1],
            r.z_ss.at[unit],
            r.z_rs.at[unit],
            device(x, y, (z + k) % NZ, core),
        )

    def z_all(unit):
        return send(
            r.z_send.at[unit],
            r.z_recv.at[unit],
            r.z_ss.at[unit],
            r.z_rs.at[unit],
            device(x, y, (z + 1) % NZ, core),
        )

    def t_copy(unit):
        away, which = PLACES[unit]
        return send(
            r.t_send.at[unit],
            r.grad.at[which, x],
            r.t_ss.at[unit],
            r.t_rs.at[which, x],
            device(y, (y + away) % NY, z, core),
        )

    def stage0(unit):
        have(unit)

        def store(i, product):
            r.core_send[unit, pl.ds(2 * i, 2)] = product.astype(bf16)

        multiply(other, unit, store)
        core_copy(unit).start()

    def own(unit):
        if unit == 0:
            turn(core)

        def store(i, product):
            r.mine[pl.ds(2 * i, 2)] = product

        multiply(core, unit, store)

    def stage1(unit):
        core_copy(unit).wait()
        if unit in Z_UNITS:
            at_unit = Z_UNITS.index(unit)
            for side in range(2):
                for at in range(2):
                    block = 2 * (2 * side + at) + 1 - z % 2
                    r.a_send[at_unit, side, at] = (
                        r.mine[block] + r.core_recv[unit, block].astype(f32)
                    ).astype(bf16)
                a_copy(unit, side).start()
            for side in range(2):
                for at in range(2):
                    block = 2 * (2 * side + at) + z % 2
                    r.a_keep[at_unit, side, at] = r.mine[block] + r.core_recv[
                        unit, block
                    ].astype(f32)

        else:
            for side in range(2):
                partner = first_partner[side]
                away = (partner, (3 - partner, partner + 1 - 2 * (partner % 2))[side])
                for k in range(2):
                    for at in range(4):
                        row_block = side * 4 + at
                        r.x1_send[unit, side, k, at] = (
                            r.mine[row_block, away[k]]
                            + r.core_recv[unit, row_block, away[k]].astype(f32)
                        ).astype(bf16)
                x1_copy(unit, side).start()
            for side in range(2):
                near = (x, second_partner[side])
                for k in range(2):
                    for at in range(4):
                        row_block = side * 4 + at
                        r.keep[unit, side, k, at] = r.mine[row_block, near[k]] + r.core_recv[
                            unit, row_block, near[k]
                        ].astype(f32)

    def a_copy(unit, side):
        return send(
            r.a_send.at[Z_UNITS.index(unit), side],
            r.a_recv.at[Z_UNITS.index(unit), side],
            r.a_ss.at[Z_UNITS.index(unit), side],
            r.a_rs.at[Z_UNITS.index(unit), side],
            device(x, y, (z + 1 - 2 * (z % 2), (z + 7 + 2 * (z % 2)) % NZ)[side], core),
        )

    def b_copy(unit, side):
        return send(
            r.b_send.at[Z_UNITS.index(unit), side],
            r.b_recv.at[Z_UNITS.index(unit), side],
            r.b_ss.at[Z_UNITS.index(unit), side],
            r.b_rs.at[Z_UNITS.index(unit), side],
            device(first_partner[side], y, z, core),
        )

    def c_copy(unit, side):
        return send(
            r.c_send.at[Z_UNITS.index(unit), side],
            r.c_recv.at[Z_UNITS.index(unit), side],
            r.c_ss.at[Z_UNITS.index(unit), side],
            r.c_rs.at[Z_UNITS.index(unit), side],
            device(second_partner[side], y, z, core),
        )

    def d_copy(unit, k):
        return send(
            r.d_send.at[Z_UNITS.index(unit), k - 1],
            r.d_recv.at[Z_UNITS.index(unit), k - 1],
            r.d_ss.at[Z_UNITS.index(unit)],
            r.d_rs.at[Z_UNITS.index(unit)],
            device(x, y, (z + 2 * k) % NZ, core),
        )

    def d_all(unit):
        return send(
            r.d_send.at[Z_UNITS.index(unit)],
            r.d_recv.at[Z_UNITS.index(unit)],
            r.d_ss.at[Z_UNITS.index(unit)],
            r.d_rs.at[Z_UNITS.index(unit)],
            device(x, y, (z + 2) % NZ, core),
        )

    def away_and_near(side):
        partner = first_partner[side]
        away = (partner, (3 - partner, partner + 1 - 2 * (partner % 2))[side])
        return away, (x, second_partner[side])

    def z_stage2(unit):
        at_unit = Z_UNITS.index(unit)
        for side in range(2):
            a_copy(unit, side).wait()
            away, near = away_and_near(side)
            for k in range(2):
                for at in range(2):
                    r.b_send[at_unit, side, k, at] = (
                        r.a_keep[at_unit, side, at, away[k]]
                        + r.a_recv[at_unit, side, at, away[k]].astype(f32)
                    ).astype(bf16)
            b_copy(unit, side).start()
            for k in range(2):
                for at in range(2):
                    r.b_keep[at_unit, side, k, at] = r.a_keep[
                        at_unit, side, at, near[k]
                    ] + r.a_recv[at_unit, side, at, near[k]].astype(f32)

    def z_stage3(unit):
        at_unit = Z_UNITS.index(unit)
        for side in range(2):
            b_copy(unit, side).wait()
            r.c_send[at_unit, side] = (
                r.b_keep[at_unit, side, 1] + r.b_recv[at_unit, side, 1].astype(f32)
            ).astype(bf16)
            c_copy(unit, side).start()
            r.b_keep[at_unit, side, 0] += r.b_recv[at_unit, side, 0].astype(f32)

    def z_stage4(unit):
        at_unit = Z_UNITS.index(unit)
        for side in range(2):
            c_copy(unit, side).wait()
            for at in range(2):
                r.d_sum[side * 2 + at] = r.b_keep[at_unit, side, 0, at] + r.c_recv[
                    at_unit, side, at
                ].astype(f32)
        for k in (2, 1, 3):
            r.d_send[at_unit, k - 1] = r.d_sum[(z // 2 + k) % 4].astype(bf16)
            d_copy(unit, k).start()
        r.z_own[unit] = r.d_sum[z // 2]

    def z_stage5(unit):
        d_all(unit).wait()
        total = r.z_own[unit]
        for k in range(3):
            total = total + r.d_recv[Z_UNITS.index(unit), k].astype(f32)
        finish(unit, total)

    def stage2(unit):
        for side in range(2):
            x1_copy(unit, side).wait()
            r.x2_send[unit, side] = (
                r.keep[unit, side, 1] + r.x1_recv[unit, side, 1].astype(f32)
            ).astype(bf16)
            x2_copy(unit, side).start()
        for side in range(2):
            r.keep[unit, side, 0] += r.x1_recv[unit, side, 0].astype(f32)

    def stage3(unit):
        for side in range(2):
            x2_copy(unit, side).wait()
            for at in range(4):
                r.z_sum[side * 4 + at] = r.keep[unit, side, 0, at] + r.x2_recv[
                    unit, side, at
                ].astype(f32)
        for k in (4, 3, 5, 2, 6, 1, 7):
            r.z_send[unit, k - 1] = r.z_sum[(z + k) % NZ].astype(bf16)
            z_copy(unit, k).start()
        r.z_own[unit] = r.z_sum[z]

    def stage4(unit):
        z_all(unit).wait()
        total = r.z_own[unit]
        for k in range(NZ - 1):
            total = total + r.z_recv[unit, k].astype(f32)
        finish(unit, total)

    def finish(unit, total):
        away, which = PLACES[unit]

        def go():
            r.t_send[unit] = total
            t_copy(unit).start()

        if away == 0:

            @pl.when(x == y)
            def _():
                r.grad[which, x] = total

            pl.when(x != y)(go)
        else:
            go()

    def xx_copy(k):
        return send(
            r.xx_send.at[k - 1],
            r.xx_recv.at[k - 1],
            r.xx_ss.at[k - 1],
            r.xx_rs.at[k - 1],
            device((x + k) % NX, y, z, core),
        )

    def xz_copy(k, source, target):
        return send(
            source,
            target,
            r.xz_sem.at[0],
            r.xz_sem.at[1],
            device(x, y, (z + k) % NZ, core),
        )

    def spread_x(_):
        x_swap.wait()
        for k in (2, 1, 3, 0):
            target = r.xx_own if k == 0 else r.xx_send.at[k - 1]
            for block in range(NZ):
                at = (x + k) % NX * NZ + block
                mine, pair = r.x_mine[core, at], r.x_pair[at]
                low, high = jnp.where(core == 0, mine, pair), jnp.where(core == 0, pair, mine)
                target[block] = jnp.concatenate([low, high], axis=0).astype(bf16)
            if k > 0:
                xx_copy(k).start()

    def spread_z(_):
        for k in range(1, NX):
            xx_copy(k).wait()
        for k in (4, 3, 5, 2, 6, 1, 7):
            to = (z + k) % NZ
            r.xz_send[k - 1, 0] = r.xx_own[to]
            for j in range(1, NX):
                r.xz_send[k - 1, j] = r.xx_recv[j - 1, to]
            xz_copy(k, r.xz_send.at[k - 1], r.xz_recv.at[k - 1]).start()

    def spread_done():
        xz_copy(1, r.xz_send, r.xz_recv).wait()
        r.x_all[0, z] = r.xx_own[z]
        for j in range(1, NX):
            r.x_all[j, z] = r.xx_recv[j - 1, z]
        for k in range(1, NZ):
            for j in range(NX):
                r.x_all[j, (z + NZ - k) % NZ] = r.xz_recv[k - 1, j]
        for k in range(4, 7):
            loads[k].wait()

    chunk = min(1024, slots)

    def cached(pair):
        row, kv_head = pair // 2, pair % 2
        if pair == 0:
            loads[3].wait()
            loads[7].wait()
            asked = jnp.concatenate([r.q_in[s].astype(f32) for s in range(4)], axis=0)
            for h in range(2):
                for g in range(8):
                    r.query[h, :, g, :] = asked[:, (h * 8 + g) * head : (h * 8 + g + 1) * head]
        query = r.query[kv_head].reshape(4, 2, 8, head)
        query = query[:, row].reshape(32, head).astype(bf16)

        def score(i, highest):
            at = pl.ds(pl.multiple_of(i * chunk, chunk), chunk)
            value = lax.dot_general(
                query,
                r.kv[0, row, kv_head, at],
                (((1,), (1,)), ((), ())),
                preferred_element_type=f32,
            )
            places = i * chunk + lax.broadcasted_iota(jnp.int32, value.shape, 1)
            value = jnp.where(places < lengths[row], value * scale, -jnp.inf)
            r.scores[:, at] = value
            return jnp.maximum(highest, jnp.max(value, axis=1, keepdims=True))

        highest = lax.fori_loop(0, slots // chunk, score, jnp.full((32, 1), -jnp.inf, f32))

        def weigh(i, carry):
            total, result = carry
            at = pl.ds(pl.multiple_of(i * chunk, chunk), chunk)
            weight = jnp.exp(r.scores[:, at] - highest)
            total = total + jnp.sum(weight, axis=1, keepdims=True)
            result = result + jnp.dot(
                weight.astype(bf16), r.kv[1, row, kv_head, at], preferred_element_type=f32
            )
            return total, result

        total, result = lax.fori_loop(
            0, slots // chunk, weigh, (jnp.zeros((32, 1), f32), jnp.zeros((32, head), f32))
        )
        highest = jnp.broadcast_to(highest, (32, head))
        total = jnp.broadcast_to(total, (32, head))
        for s in range(4):
            at = pl.ds(s * 16 + row * 8, 8)
            one = slice(s * 8, s * 8 + 8)
            r.att[kv_head, at] = result[one]
            r.top[kv_head, at] = highest[one]
            r.total[kv_head, at] = total[one]

    def store_copy(which, s):
        return pltpu.make_async_copy(
            r.grad.at[which, s],
            grad_out.at[pl.ds(s * part, part), pl.ds(which * half, half)],
            r.out_sem.at[which, s],
        )

    def yc_copy(which, k):
        return send(
            r.y_part.at[which, k, :, other],
            r.y_core.at[which, k],
            r.yc_ss.at[which, k],
            r.yc_rs.at[which, k],
            device(x, y, z, other),
        )

    def yx_copy(which, k):
        return send(
            r.yx_send.at[which, k - 1],
            r.yx_recv.at[which, k - 1],
            r.yx_ss.at[which, k - 1],
            r.yx_rs.at[which, k - 1],
            device((x + NX - k) % NX, y, z, core),
        )

    def yz_copy(which, k):
        return send(
            r.y_sum.at[which, (z + k) % NZ],
            r.yz_recv.at[which, k - 1],
            r.yz_sem.at[which, 0],
            r.yz_sem.at[which, 1],
            device(x, y, (z + k) % NZ, core),
        )

    def new0(which):
        if which == first_head:
            spread_done()
        for s in range(4):

            @pl.when(jnp.logical_or(x != y, x != s))
            def _():
                send(
                    r.t_send.at[0],
                    r.grad.at[which, s],
                    r.t_ss.at[0],
                    r.t_rs.at[which, s],
                    device(x, (y + 1) % NY, z, core),
                ).wait_recv()

            at = (pl.ds(s * part, part), pl.ds(which * half, half))
            master, _, _ = adam(r.grad[which, s], *(r.state[i, at[0], at[1]] for i in range(3)))
            r.rollout[at[0], at[1]] = master.astype(bf16)
        for k in (2, 1, 3, 0):
            product = jnp.dot(
                r.x_all[k].reshape(NZ * 16, rows),
                r.rollout[:, which * half : (which + 1) * half],
                preferred_element_type=f32,
            )
            r.y_part[which, k] = product.reshape(NZ, 2, 8, half)
            yc_copy(which, k).start()
        for s in range(4):
            store_copy(which, s).start()

    def new1(which):
        for k in (2, 1, 3):
            yc_copy(which, k).wait()
            r.yx_send[which, k - 1] = r.y_part[which, k, :, core] + r.y_core[which, k]
            yx_copy(which, k).start()
        yc_copy(which, 0).wait()
        r.y_sum[which] = r.y_part[which, 0, :, core] + r.y_core[which, 0]

    def new2(which):
        for k in (1, 3, 2):
            yx_copy(which, k).wait()
            r.y_sum[which] += r.yx_recv[which, k - 1]
        for k in (4, 3, 5, 2, 6, 1, 7):
            yz_copy(which, k).start()

    def new3(which):
        send(
            r.y_sum.at[which, pl.ds(0, NZ - 1)],
            r.yz_recv.at[which],
            r.yz_sem.at[which, 0],
            r.yz_sem.at[which, 1],
            device(x, y, (z + 1) % NZ, core),
        ).wait()
        fresh = r.y_sum[which, z]
        for k in range(NZ - 1):
            fresh = fresh + r.yz_recv[which, k]
        for s in range(4):
            new_out[s, :, pl.ds(which * half, half)] = fresh[2 * s : 2 * s + 2].astype(bf16)
        fresh = fresh.astype(bf16)
        key, value = fresh[:, :head], fresh[:, head:]
        line = lax.broadcasted_iota(jnp.int32, (64, 8), 0)
        spot = lax.broadcasted_iota(jnp.int32, (64, 8), 1)
        allowed = jnp.logical_and((line // 8) % 2 == spot % 2, spot // 2 <= line // 16)
        score = lax.dot_general(
            r.query[which].reshape(64, head).astype(bf16),
            key,
            (((1,), (1,)), ((), ())),
            preferred_element_type=f32,
        )
        score = jnp.where(allowed, score * scale, -jnp.inf)
        before = r.top[which][:, :1]
        highest = jnp.maximum(before, jnp.max(score, axis=1, keepdims=True))
        weight = jnp.exp(score - highest)
        factor = jnp.exp(before - highest)
        total = r.total[which][:, :1] * factor + jnp.sum(weight, axis=1, keepdims=True)
        result = r.att[which] * factor + jnp.dot(
            weight.astype(bf16), value, preferred_element_type=f32
        )
        r.answer[which] = (result / total).reshape(8, 8, head)
        for g in range(8):
            value = r.answer[which, :, g, :]
            at = pl.ds((which * 8 + g) * head, head)
            for s in range(4):
                att_out[s, :, at] = value[2 * s : 2 * s + 2].astype(bf16)

    steps = dict(
        F=forward,
        X=spread_x,
        Y=spread_z,
        A=cached,
        B=stage0,
        C=own,
        D=stage1,
        E=stage2,
        G=stage3,
        H=stage4,
        I=z_stage2,
        J=z_stage3,
        K=z_stage4,
        L=z_stage5,
        P=new0,
        Q=new1,
        R=new2,
        S=new3,
    )
    order = [(word[0], int(word[1])) for word in ORDER]
    first_head = [place for name, place in order if name == NEW][0]
    turn(other)
    for name, place in order:
        steps[name](place)
    for unit in range(UNITS):
        if PLACES[unit][0] == 0:
            pl.when(x != y)(lambda: t_copy(unit).wait_send())
        else:
            t_copy(unit).wait_send()
    for index in range(6):
        cot_copy(index).wait_send()
    for which in range(2):
        for s in range(4):
            store_copy(which, s).wait()


def last(gradient, master, first, second, new_kv, attended, *results):
    values = (*adam(gradient[...], master[...], first[...], second[...]), new_kv[...], attended[...])
    for result, value in zip(results, values):
        result[...] = value


def shards(
    features,
    kv_cotangent,
    master_weight,
    first_moment,
    second_moment,
    decode_inputs,
    queries,
    kv_cache,
    cache_lengths,
):
    tokens = features.shape[0]
    rows, columns = master_weight.shape
    steps, own_rows, width = decode_inputs.shape
    heads, slots, head = kv_cache.shape[2:]
    shapes = scratch(rows, columns, tokens, slots, head)
    in_vmem = pl.BlockSpec(memory_space=pltpu.VMEM)
    anywhere = pl.BlockSpec(memory_space=pl.ANY)
    gradient, new_kv, attended = pl.pallas_call(
        functools.partial(kernel, tuple(shapes)),
        out_shape=(
            jax.ShapeDtypeStruct((rows, columns), f32),
            jax.ShapeDtypeStruct((steps, own_rows, columns), bf16),
            jax.ShapeDtypeStruct(queries.shape, bf16),
        ),
        in_specs=[pl.BlockSpec(memory_space=pltpu.SMEM)] + [anywhere] * 8,
        out_specs=(anywhere, in_vmem, in_vmem),
        scratch_shapes=list(shapes.values()),
        compiler_params=pltpu.CompilerParams(
            collective_id=0, has_side_effects=True, vmem_limit_bytes=56 * 2**20
        ),
        name="fused_step",
    )(
        cache_lengths,
        queries,
        decode_inputs,
        features,
        kv_cotangent,
        master_weight,
        first_moment,
        second_moment,
        kv_cache,
    )
    like = jax.ShapeDtypeStruct((rows, columns), f32)
    return pl.pallas_call(
        last,
        out_shape=(
            like,
            like,
            like,
            jax.ShapeDtypeStruct(new_kv.shape, bf16),
            jax.ShapeDtypeStruct(attended.shape, bf16),
        ),
        in_specs=[in_vmem] * 6,
        out_specs=[in_vmem] * 5,
        name="last",
    )(gradient, master_weight, first_moment, second_moment, new_kv, attended)


def solution(mesh):
    in_specs = (
        P(("learn", "dp"), "tp"),
        P(("learn", "dp"), "tp"),
        P(("learn", "dp"), "tp"),
        P(("learn", "dp"), "tp"),
        P(("learn", "dp"), "tp"),
        P(None, ("learn", "dp"), None),
        P(None, ("learn", "dp"), "tp"),
        P(None, ("learn", "dp"), "tp", None, None),
        P(("learn", "dp")),
    )
    out_specs = (
        P(("learn", "dp"), "tp"),
        P(("learn", "dp"), "tp"),
        P(("learn", "dp"), "tp"),
        P(None, ("learn", "dp"), "tp"),
        P(None, ("learn", "dp"), "tp"),
    )
    return jax.shard_map(shards, mesh=mesh, in_specs=in_specs, out_specs=out_specs, check_vma=False)
```

```python
import functools
import types

import jax
import jax.numpy as jnp
from jax import lax
from jax.experimental import pallas as pl
from jax.experimental.pallas import tpu as pltpu
from jax.sharding import PartitionSpec as P

learn_rate = 0.005
decay_rate = 0.1
first_fix = 1.0 - 0.9**10
second_fix = 1.0 - 0.999**10

MESH = pl.DeviceIdType.MESH
UNITS = 8
NX, NY, NZ = 4, 4, 8
PLACES = ((0, 0), (0, 1), (1, 0), (3, 0), (1, 1), (3, 1), (2, 0), (2, 1))
Z_UNITS = (1, 2, 4, 6, 7)
ORDER = (
    "B0", "B1", "X0", "C0", "D0", "C1", "D1", "Y0", "A0", "F0", "B2", "B3",
    "E0", "C2", "A1", "I1", "D2", "C3", "F1", "G0", "B4", "B5", "D3", "C4",
    "J1", "A2", "I2", "D4", "B6", "C5", "D5", "C6", "E3", "K1", "B7", "H0",
    "D6", "J2", "C7", "I4", "A3", "D7", "E5", "L1", "G3", "K2", "I6", "J4",
    "I7", "G5", "J6", "K4", "J7", "H3", "K6", "L2", "K7", "H5", "L4", "L6",
    "L7", "P0", "P1", "Q0", "Q1", "R0", "R1", "S0", "S1",
)

bf16 = jnp.bfloat16
f32 = jnp.float32


def position():
    learn, dp = lax.axis_index("learn"), lax.axis_index("dp")
    return learn // 4, lax.axis_index("tp"), (learn % 4) * 2 + dp // 2, dp % 2


def device(x, y, z, core):
    return {"learn": x * 4 + z // 2, "tp": y, "dp": (z % 2) * 2 + core}


def send(source, target, send_sem, recv_sem, where):
    return pltpu.make_async_remote_copy(
        src_ref=source,
        dst_ref=target,
        send_sem=send_sem,
        recv_sem=recv_sem,
        device_id=where,
        device_id_type=MESH,
    )


def adam(gradient, master, first, second):
    first = 0.9 * first + 0.1 * gradient
    second = 0.999 * second + 0.001 * gradient * gradient
    update = (first / first_fix) / (jnp.sqrt(second / second_fix) + 1e-08)
    return master - learn_rate * (update + decay_rate * master), first, second


def scratch(rows, columns, tokens, slots, head):
    part, half = rows // 4, columns // 2
    dma = pltpu.SemaphoreType.DMA
    return dict(
        feat=pltpu.VMEM((tokens, 16 * rows), bf16),
        turned=pltpu.VMEM((2, NZ, rows, tokens), bf16),
        cot=pltpu.VMEM((UNITS, tokens, half), bf16),
        core_send=pltpu.VMEM((UNITS, NZ, 4, part, half), bf16),
        core_recv=pltpu.VMEM((UNITS, NZ, 4, part, half), bf16),
        mine=pltpu.VMEM((NZ, 4, part, half), f32),
        keep=pltpu.VMEM((UNITS, 2, 2, 4, part, half), f32),
        x1_send=pltpu.VMEM((UNITS, 2, 2, 4, part, half), bf16),
        x1_recv=pltpu.VMEM((UNITS, 2, 2, 4, part, half), bf16),
        x2_send=pltpu.VMEM((UNITS, 2, 4, part, half), bf16),
        x2_recv=pltpu.VMEM((UNITS, 2, 4, part, half), bf16),
        a_send=pltpu.VMEM((max(1, len(Z_UNITS)), 2, 2, 4, part, half), bf16),
        a_recv=pltpu.VMEM((max(1, len(Z_UNITS)), 2, 2, 4, part, half), bf16),
        a_keep=pltpu.VMEM((max(1, len(Z_UNITS)), 2, 2, 4, part, half), f32),
        b_keep=pltpu.VMEM((max(1, len(Z_UNITS)), 2, 2, 2, part, half), f32),
        b_send=pltpu.VMEM((max(1, len(Z_UNITS)), 2, 2, 2, part, half), bf16),
        b_recv=pltpu.VMEM((max(1, len(Z_UNITS)), 2, 2, 2, part, half), bf16),
        c_send=pltpu.VMEM((max(1, len(Z_UNITS)), 2, 2, part, half), bf16),
        c_recv=pltpu.VMEM((max(1, len(Z_UNITS)), 2, 2, part, half), bf16),
        d_sum=pltpu.VMEM((4, part, half), f32),
        d_send=pltpu.VMEM((max(1, len(Z_UNITS)), 3, part, half), bf16),
        d_recv=pltpu.VMEM((max(1, len(Z_UNITS)), 3, part, half), bf16),
        a_ss=dma((max(1, len(Z_UNITS)), 2)),
        a_rs=dma((max(1, len(Z_UNITS)), 2)),
        b_ss=dma((max(1, len(Z_UNITS)), 2)),
        b_rs=dma((max(1, len(Z_UNITS)), 2)),
        c_ss=dma((max(1, len(Z_UNITS)), 2)),
        c_rs=dma((max(1, len(Z_UNITS)), 2)),
        d_ss=dma((max(1, len(Z_UNITS)),)),
        d_rs=dma((max(1, len(Z_UNITS)),)),
        z_sum=pltpu.VMEM((NZ, part, half), f32),
        z_own=pltpu.VMEM((UNITS, part, half), f32),
        z_send=pltpu.VMEM((UNITS, NZ - 1, part, half), bf16),
        z_recv=pltpu.VMEM((UNITS, NZ - 1, part, half), bf16),
        t_send=pltpu.VMEM((UNITS, part, half), f32),
        grad=pltpu.VMEM((2, 4, part, half), f32),
        kv=pltpu.VMEM((2, 2, 2, slots, head), bf16),
        state=pltpu.VMEM((3, rows, columns), f32),
        rollout=pltpu.VMEM((rows, columns), bf16),
        q_in=pltpu.VMEM((4, 2, 16 * head), bf16),
        x_in=pltpu.VMEM((4, 2, 64 * rows), bf16),
        x_mine=pltpu.VMEM((2, 32, 8, rows), f32),
        x_pair=pltpu.VMEM((32, 8, rows), f32),
        xz_send=pltpu.VMEM((NZ - 1, NX, 16, rows), bf16),
        xz_recv=pltpu.VMEM((NZ - 1, NX, 16, rows), bf16),
        xx_send=pltpu.VMEM((NX - 1, NZ, 16, rows), bf16),
        xx_recv=pltpu.VMEM((NX - 1, NZ, 16, rows), bf16),
        xx_own=pltpu.VMEM((NZ, 16, rows), bf16),
        x_all=pltpu.VMEM((NX, NZ, 16, rows), bf16),
        y_part=pltpu.VMEM((2, NX, NZ, 2, 8, half), f32),
        y_core=pltpu.VMEM((2, NX, NZ, 8, half), f32),
        yx_send=pltpu.VMEM((2, NX - 1, NZ, 8, half), f32),
        yx_recv=pltpu.VMEM((2, NX - 1, NZ, 8, half), f32),
        y_sum=pltpu.VMEM((2, NZ, 8, half), f32),
        yz_recv=pltpu.VMEM((2, NZ - 1, 8, half), f32),
        scores=pltpu.VMEM((32, slots), f32),
        query=pltpu.VMEM((2, 8, 8, head), f32),
        answer=pltpu.VMEM((2, 8, 8, head), f32),
        att=pltpu.VMEM((2, 64, head), f32),
        top=pltpu.VMEM((2, 64, head), f32),
        total=pltpu.VMEM((2, 64, head), f32),
        load_sem=dma((9,)),
        out_sem=dma((2, 4)),
        cot_ss=dma((6,)),
        cot_rs=dma((UNITS,)),
        core_ss=dma((UNITS,)),
        core_rs=dma((UNITS,)),
        x1_ss=dma((UNITS, 2)),
        x1_rs=dma((UNITS, 2)),
        x2_ss=dma((UNITS, 2)),
        x2_rs=dma((UNITS, 2)),
        z_ss=dma((UNITS,)),
        z_rs=dma((UNITS,)),
        t_ss=dma((UNITS,)),
        t_rs=dma((2, 4)),
        xc_sem=dma((2,)),
        xz_sem=dma((2,)),
        xx_ss=dma((3,)),
        xx_rs=dma((3,)),
        yc_ss=dma((2, 4)),
        yc_rs=dma((2, 4)),
        yx_ss=dma((2, 3)),
        yx_rs=dma((2, 3)),
        yz_sem=dma((2, 2)),
    )


def kernel(names, *refs):
    (lengths, q_hbm, x_hbm, f_hbm, c_hbm, w_hbm, m_hbm, v_hbm, kv_hbm) = refs[:9]
    (grad_out, new_out, att_out) = refs[9:12]
    r = types.SimpleNamespace(**dict(zip(names, refs[12:])))
    x, y, z, core = position()
    other = 1 - core
    flip, mirror = x + 1 - 2 * (x % 2), 3 - x
    first_partner, second_partner = (flip, mirror), (mirror, flip)
    rows, columns = r.rollout.shape
    part, half = rows // 4, columns // 2
    tokens = r.feat.shape[0]
    slots, head = r.kv.shape[3:]
    scale = head**-0.5

    loads = [
        pltpu.make_async_copy(source, target, r.load_sem.at[i])
        for i, (source, target) in enumerate(
            (
                (c_hbm.at[:, pl.ds(0, half)], r.cot.at[0]),
                (f_hbm, r.feat),
                (c_hbm.at[:, pl.ds(half, half)], r.cot.at[1]),
                (kv_hbm, r.kv),
                (w_hbm, r.state.at[0]),
                (m_hbm, r.state.at[1]),
                (v_hbm, r.state.at[2]),
                (q_hbm, r.q_in),
                (x_hbm, r.x_in),
            )
        )
    ]
    for index in (1, 0, 2, 8):
        loads[index].start()

    barrier = pltpu.get_barrier_semaphore()

    def greet(where):
        pl.semaphore_signal(barrier, inc=1, device_id=where, device_id_type=MESH)

    greet(device(x, y, z, other))
    for k in range(1, NX):
        greet(device((x + k) % NX, y, z, core))
    for k in range(1, NZ):
        greet(device(x, y, (z + k) % NZ, core))
    for k in range(1, NY):
        greet(device(x, (y + k) % NY, z, core))
    for k in range(4):

        @pl.when(jnp.logical_or(x != y, y != k))
        def _():
            greet(device(y, k, z, core))

        @pl.when(jnp.logical_or(x != y, x != k))
        def _():
            greet(device(k, x, z, core))

    same = (4 - (x - y + 4) % 4) // 4
    pl.semaphore_wait(barrier, 1 + (NX - 1) + (NZ - 1) + (NY - 1) + 8 - 2 * same)

    slot = {place: unit for unit, place in enumerate(PLACES)}
    arrived = {slot[0, 0]}

    def cot_copy(index):
        step = (3, 1, 3, 1, 1, 3)[index]
        half_of = (0, 0, 1, 1, 0, 1)[index]
        source = slot[0, half_of] if index < 4 else slot[(3, 1)[half_of], half_of]
        target = slot[4 - step, half_of] if index < 4 else slot[2, half_of]
        start = c_hbm.at[:, pl.ds(half_of * half, half)] if index < 4 else r.cot.at[source]
        return send(
            start,
            r.cot.at[target],
            r.cot_ss.at[index],
            r.cot_rs.at[target],
            device(x, (y + step) % NY, z, core),
        )

    def have(unit):
        if unit == slot[0, 1] and unit not in arrived:
            loads[2].wait()
        elif unit not in arrived:
            send(
                r.cot.at[unit],
                r.cot.at[unit],
                r.cot_ss.at[0],
                r.cot_rs.at[unit],
                device(x, (y + 1) % NY, z, core),
            ).wait_recv()
        arrived.add(unit)

    def forward(part_of):
        have(slot[(3, 1)[part_of], part_of])
        cot_copy(4 + part_of).start()

    x_swap = send(
        r.x_mine.at[other],
        r.x_pair,
        r.xc_sem.at[0],
        r.xc_sem.at[1],
        device(x, y, z, other),
    )
    for index in range(4):
        cot_copy(index).start()
    loads[8].wait()
    inputs = jnp.concatenate([r.x_in[s].astype(f32) for s in range(4)], axis=0)
    for block in range(64):
        r.x_mine[block % 2, block // 2] = inputs[:, block * rows : (block + 1) * rows]
    x_swap.start()
    loads[0].wait()
    loads[1].wait()
    for index in range(3, 8):
        loads[index].start()

    def turn(side):
        for row_block in range(NZ):
            columns_of = pl.ds(pl.multiple_of((row_block * 2 + side) * rows, rows), rows)
            r.turned[side, row_block] = r.feat[:, columns_of].T

    def multiply(side, unit, store):
        def step(i, carry):
            left = r.turned[side, pl.ds(2 * i, 2)].reshape(2 * rows, tokens)
            product = jnp.dot(left, r.cot[unit], preferred_element_type=f32)
            store(i, product.reshape(2, 4, part, half))
            return carry

        lax.fori_loop(0, NZ // 2, step, 0, unroll=True)

    def core_copy(unit):
        return send(
            r.core_send.at[unit],
            r.core_recv.at[unit],
            r.core_ss.at[unit],
            r.core_rs.at[unit],
            device(x, y, z, other),
        )

    def x1_copy(unit, side):
        return send(
            r.x1_send.at[unit, side],
            r.x1_recv.at[unit, side],
            r.x1_ss.at[unit, side],
            r.x1_rs.at[unit, side],
            device(first_partner[side], y, z, core),
        )

    def x2_copy(unit, side):
        return send(
            r.x2_send.at[unit, side],
            r.x2_recv.at[unit, side],
            r.x2_ss.at[unit, side],
            r.x2_rs.at[unit, side],
            device(second_partner[side], y, z, core),
        )

    def z_copy(unit, k):
        return send(
            r.z_send.at[unit, k - 1],
            r.z_recv.at[unit, k - 1],
            r.z_ss.at[unit],
            r.z_rs.at[unit],
            device(x, y, (z + k) % NZ, core),
        )

    def z_all(unit):
        return send(
            r.z_send.at[unit],
            r.z_recv.at[unit],
            r.z_ss.at[unit],
            r.z_rs.at[unit],
            device(x, y, (z + 1) % NZ, core),
        )

    def t_copy(unit):
        away, which = PLACES[unit]
        return send(
            r.t_send.at[unit],
            r.grad.at[which, x],
            r.t_ss.at[unit],
            r.t_rs.at[which, x],
            device(y, (y + away) % NY, z, core),
        )

    def stage0(unit):
        have(unit)

        def store(i, product):
            r.core_send[unit, pl.ds(2 * i, 2)] = product.astype(bf16)

        multiply(other, unit, store)
        core_copy(unit).start()

    def own(unit):
        if unit == 0:
            turn(core)

        def store(i, product):
            r.mine[pl.ds(2 * i, 2)] = product

        multiply(core, unit, store)

    def stage1(unit):
        core_copy(unit).wait()
        if unit in Z_UNITS:
            at_unit = Z_UNITS.index(unit)
            for side in range(2):
                for at in range(2):
                    block = 2 * (2 * side + at) + 1 - z % 2
                    r.a_send[at_unit, side, at] = (
                        r.mine[block] + r.core_recv[unit, block].astype(f32)
                    ).astype(bf16)
                a_copy(unit, side).start()
            for side in range(2):
                for at in range(2):
                    block = 2 * (2 * side + at) + z % 2
                    r.a_keep[at_unit, side, at] = r.mine[block] + r.core_recv[
                        unit, block
                    ].astype(f32)

        else:
            for side in range(2):
                partner = first_partner[side]
                away = (partner, (3 - partner, partner + 1 - 2 * (partner % 2))[side])
                for k in range(2):
                    for at in range(4):
                        row_block = side * 4 + at
                        r.x1_send[unit, side, k, at] = (
                            r.mine[row_block, away[k]]
                            + r.core_recv[unit, row_block, away[k]].astype(f32)
                        ).astype(bf16)
                x1_copy(unit, side).start()
            for side in range(2):
                near = (x, second_partner[side])
                for k in range(2):
                    for at in range(4):
                        row_block = side * 4 + at
                        r.keep[unit, side, k, at] = r.mine[row_block, near[k]] + r.core_recv[
                            unit, row_block, near[k]
                        ].astype(f32)

    def a_copy(unit, side):
        return send(
            r.a_send.at[Z_UNITS.index(unit), side],
            r.a_recv.at[Z_UNITS.index(unit), side],
            r.a_ss.at[Z_UNITS.index(unit), side],
            r.a_rs.at[Z_UNITS.index(unit), side],
            device(x, y, (z + 1 - 2 * (z % 2), (z + 7 + 2 * (z % 2)) % NZ)[side], core),
        )

    def b_copy(unit, side):
        return send(
            r.b_send.at[Z_UNITS.index(unit), side],
            r.b_recv.at[Z_UNITS.index(unit), side],
            r.b_ss.at[Z_UNITS.index(unit), side],
            r.b_rs.at[Z_UNITS.index(unit), side],
            device(first_partner[side], y, z, core),
        )

    def c_copy(unit, side):
        return send(
            r.c_send.at[Z_UNITS.index(unit), side],
            r.c_recv.at[Z_UNITS.index(unit), side],
            r.c_ss.at[Z_UNITS.index(unit), side],
            r.c_rs.at[Z_UNITS.index(unit), side],
            device(second_partner[side], y, z, core),
        )

    def d_copy(unit, k):
        return send(
            r.d_send.at[Z_UNITS.index(unit), k - 1],
            r.d_recv.at[Z_UNITS.index(unit), k - 1],
            r.d_ss.at[Z_UNITS.index(unit)],
            r.d_rs.at[Z_UNITS.index(unit)],
            device(x, y, (z + 2 * k) % NZ, core),
        )

    def d_all(unit):
        return send(
            r.d_send.at[Z_UNITS.index(unit)],
            r.d_recv.at[Z_UNITS.index(unit)],
            r.d_ss.at[Z_UNITS.index(unit)],
            r.d_rs.at[Z_UNITS.index(unit)],
            device(x, y, (z + 2) % NZ, core),
        )

    def away_and_near(side):
        partner = first_partner[side]
        away = (partner, (3 - partner, partner + 1 - 2 * (partner % 2))[side])
        return away, (x, second_partner[side])

    def z_stage2(unit):
        at_unit = Z_UNITS.index(unit)
        for side in range(2):
            a_copy(unit, side).wait()
            away, near = away_and_near(side)
            for k in range(2):
                for at in range(2):
                    r.b_send[at_unit, side, k, at] = (
                        r.a_keep[at_unit, side, at, away[k]]
                        + r.a_recv[at_unit, side, at, away[k]].astype(f32)
                    ).astype(bf16)
            b_copy(unit, side).start()
            for k in range(2):
                for at in range(2):
                    r.b_keep[at_unit, side, k, at] = r.a_keep[
                        at_unit, side, at, near[k]
                    ] + r.a_recv[at_unit, side, at, near[k]].astype(f32)

    def z_stage3(unit):
        at_unit = Z_UNITS.index(unit)
        for side in range(2):
            b_copy(unit, side).wait()
            r.c_send[at_unit, side] = (
                r.b_keep[at_unit, side, 1] + r.b_recv[at_unit, side, 1].astype(f32)
            ).astype(bf16)
            c_copy(unit, side).start()
            r.b_keep[at_unit, side, 0] += r.b_recv[at_unit, side, 0].astype(f32)

    def z_stage4(unit):
        at_unit = Z_UNITS.index(unit)
        for side in range(2):
            c_copy(unit, side).wait()
            for at in range(2):
                r.d_sum[side * 2 + at] = r.b_keep[at_unit, side, 0, at] + r.c_recv[
                    at_unit, side, at
                ].astype(f32)
        for k in (2, 1, 3):
            r.d_send[at_unit, k - 1] = r.d_sum[(z // 2 + k) % 4].astype(bf16)
            d_copy(unit, k).start()
        r.z_own[unit] = r.d_sum[z // 2]

    def z_stage5(unit):
        d_all(unit).wait()
        total = r.z_own[unit]
        for k in range(3):
            total = total + r.d_recv[Z_UNITS.index(unit), k].astype(f32)
        finish(unit, total)

    def stage2(unit):
        for side in range(2):
            x1_copy(unit, side).wait()
            r.x2_send[unit, side] = (
                r.keep[unit, side, 1] + r.x1_recv[unit, side, 1].astype(f32)
            ).astype(bf16)
            x2_copy(unit, side).start()
        for side in range(2):
            r.keep[unit, side, 0] += r.x1_recv[unit, side, 0].astype(f32)

    def stage3(unit):
        for side in range(2):
            x2_copy(unit, side).wait()
            for at in range(4):
                r.z_sum[side * 4 + at] = r.keep[unit, side, 0, at] + r.x2_recv[
                    unit, side, at
                ].astype(f32)
        for k in (4, 3, 5, 2, 6, 1, 7):
            r.z_send[unit, k - 1] = r.z_sum[(z + k) % NZ].astype(bf16)
            z_copy(unit, k).start()
        r.z_own[unit] = r.z_sum[z]

    def stage4(unit):
        z_all(unit).wait()
        total = r.z_own[unit]
        for k in range(NZ - 1):
            total = total + r.z_recv[unit, k].astype(f32)
        finish(unit, total)

    def finish(unit, total):
        away, which = PLACES[unit]

        def go():
            r.t_send[unit] = total
            t_copy(unit).start()

        if away == 0:

            @pl.when(x == y)
            def _():
                r.grad[which, x] = total

            pl.when(x != y)(go)
        else:
            go()

    def xx_copy(k):
        return send(
            r.xx_send.at[k - 1],
            r.xx_recv.at[k - 1],
            r.xx_ss.at[k - 1],
            r.xx_rs.at[k - 1],
            device((x + k) % NX, y, z, core),
        )

    def xz_copy(k, source, target):
        return send(
            source,
            target,
            r.xz_sem.at[0],
            r.xz_sem.at[1],
            device(x, y, (z + k) % NZ, core),
        )

    def spread_x(_):
        x_swap.wait()
        for k in (2, 1, 3, 0):
            target = r.xx_own if k == 0 else r.xx_send.at[k - 1]
            for block in range(NZ):
                at = (x + k) % NX * NZ + block
                mine, pair = r.x_mine[core, at], r.x_pair[at]
                low, high = jnp.where(core == 0, mine, pair), jnp.where(core == 0, pair, mine)
                target[block] = jnp.concatenate([low, high], axis=0).astype(bf16)
            if k > 0:
                xx_copy(k).start()

    def spread_z(_):
        for k in range(1, NX):
            xx_copy(k).wait()
        for k in (4, 3, 5, 2, 6, 1, 7):
            to = (z + k) % NZ
            r.xz_send[k - 1, 0] = r.xx_own[to]
            for j in range(1, NX):
                r.xz_send[k - 1, j] = r.xx_recv[j - 1, to]
            xz_copy(k, r.xz_send.at[k - 1], r.xz_recv.at[k - 1]).start()

    def spread_done():
        xz_copy(1, r.xz_send, r.xz_recv).wait()
        r.x_all[0, z] = r.xx_own[z]
        for j in range(1, NX):
            r.x_all[j, z] = r.xx_recv[j - 1, z]
        for k in range(1, NZ):
            for j in range(NX):
                r.x_all[j, (z + NZ - k) % NZ] = r.xz_recv[k - 1, j]
        for k in range(4, 7):
            loads[k].wait()

    chunk = min(1024, slots)

    def cached(pair):
        row, kv_head = pair // 2, pair % 2
        if pair == 0:
            loads[3].wait()
            loads[7].wait()
            asked = jnp.concatenate([r.q_in[s].astype(f32) for s in range(4)], axis=0)
            for h in range(2):
                for g in range(8):
                    r.query[h, :, g, :] = asked[:, (h * 8 + g) * head : (h * 8 + g + 1) * head]
        query = r.query[kv_head].reshape(4, 2, 8, head)
        query = query[:, row].reshape(32, head).astype(bf16)

        def score(i, highest):
            at = pl.ds(pl.multiple_of(i * chunk, chunk), chunk)
            value = lax.dot_general(
                query,
                r.kv[0, row, kv_head, at],
                (((1,), (1,)), ((), ())),
                preferred_element_type=f32,
            )
            places = i * chunk + lax.broadcasted_iota(jnp.int32, value.shape, 1)
            value = jnp.where(places < lengths[row], value * scale, -jnp.inf)
            r.scores[:, at] = value
            return jnp.maximum(highest, jnp.max(value, axis=1, keepdims=True))

        highest = lax.fori_loop(0, slots // chunk, score, jnp.full((32, 1), -jnp.inf, f32))

        def weigh(i, carry):
            total, result = carry
            at = pl.ds(pl.multiple_of(i * chunk, chunk), chunk)
            weight = jnp.exp(r.scores[:, at] - highest)
            total = total + jnp.sum(weight, axis=1, keepdims=True)
            result = result + jnp.dot(
                weight.astype(bf16), r.kv[1, row, kv_head, at], preferred_element_type=f32
            )
            return total, result

        total, result = lax.fori_loop(
            0, slots // chunk, weigh, (jnp.zeros((32, 1), f32), jnp.zeros((32, head), f32))
        )
        highest = jnp.broadcast_to(highest, (32, head))
        total = jnp.broadcast_to(total, (32, head))
        for s in range(4):
            at = pl.ds(s * 16 + row * 8, 8)
            one = slice(s * 8, s * 8 + 8)
            r.att[kv_head, at] = result[one]
            r.top[kv_head, at] = highest[one]
            r.total[kv_head, at] = total[one]

    def store_copy(which, s):
        return pltpu.make_async_copy(
            r.grad.at[which, s],
            grad_out.at[pl.ds(s * part, part), pl.ds(which * half, half)],
            r.out_sem.at[which, s],
        )

    def yc_copy(which, k):
        return send(
            r.y_part.at[which, k, :, other],
            r.y_core.at[which, k],
            r.yc_ss.at[which, k],
            r.yc_rs.at[which, k],
            device(x, y, z, other),
        )

    def yx_copy(which, k):
        return send(
            r.yx_send.at[which, k - 1],
            r.yx_recv.at[which, k - 1],
            r.yx_ss.at[which, k - 1],
            r.yx_rs.at[which, k - 1],
            device((x + NX - k) % NX, y, z, core),
        )

    def yz_copy(which, k):
        return send(
            r.y_sum.at[which, (z + k) % NZ],
            r.yz_recv.at[which, k - 1],
            r.yz_sem.at[which, 0],
            r.yz_sem.at[which, 1],
            device(x, y, (z + k) % NZ, core),
        )

    def new0(which):
        for s in range(4):

            @pl.when(jnp.logical_or(x != y, x != s))
            def _():
                send(
                    r.t_send.at[0],
                    r.grad.at[which, s],
                    r.t_ss.at[0],
                    r.t_rs.at[which, s],
                    device(x, (y + 1) % NY, z, core),
                ).wait_recv()

            at = (pl.ds(s * part, part), pl.ds(which * half, half))
            master, _, _ = adam(r.grad[which, s], *(r.state[i, at[0], at[1]] for i in range(3)))
            r.rollout[at[0], at[1]] = master.astype(bf16)
        for k in (2, 1, 3, 0):
            product = jnp.dot(
                r.x_all[k].reshape(NZ * 16, rows),
                r.rollout[:, which * half : (which + 1) * half],
                preferred_element_type=f32,
            )
            r.y_part[which, k] = product.reshape(NZ, 2, 8, half)
            yc_copy(which, k).start()
        for s in range(4):
            store_copy(which, s).start()

    def new1(which):
        for k in (2, 1, 3):
            yc_copy(which, k).wait()
            r.yx_send[which, k - 1] = r.y_part[which, k, :, core] + r.y_core[which, k]
            yx_copy(which, k).start()
        yc_copy(which, 0).wait()
        r.y_sum[which] = r.y_part[which, 0, :, core] + r.y_core[which, 0]

    def new2(which):
        for k in (1, 3, 2):
            yx_copy(which, k).wait()
            r.y_sum[which] += r.yx_recv[which, k - 1]
        for k in (4, 3, 5, 2, 6, 1, 7):
            yz_copy(which, k).start()

    def new3(which):
        send(
            r.y_sum.at[which, pl.ds(0, NZ - 1)],
            r.yz_recv.at[which],
            r.yz_sem.at[which, 0],
            r.yz_sem.at[which, 1],
            device(x, y, (z + 1) % NZ, core),
        ).wait()
        fresh = r.y_sum[which, z]
        for k in range(NZ - 1):
            fresh = fresh + r.yz_recv[which, k]
        for s in range(4):
            new_out[s, :, pl.ds(which * half, half)] = fresh[2 * s : 2 * s + 2].astype(bf16)
        fresh = fresh.astype(bf16)
        key, value = fresh[:, :head], fresh[:, head:]
        line = lax.broadcasted_iota(jnp.int32, (64, 8), 0)
        spot = lax.broadcasted_iota(jnp.int32, (64, 8), 1)
        allowed = jnp.logical_and((line // 8) % 2 == spot % 2, spot // 2 <= line // 16)
        score = lax.dot_general(
            r.query[which].reshape(64, head).astype(bf16),
            key,
            (((1,), (1,)), ((), ())),
            preferred_element_type=f32,
        )
        score = jnp.where(allowed, score * scale, -jnp.inf)
        before = r.top[which][:, :1]
        highest = jnp.maximum(before, jnp.max(score, axis=1, keepdims=True))
        weight = jnp.exp(score - highest)
        factor = jnp.exp(before - highest)
        total = r.total[which][:, :1] * factor + jnp.sum(weight, axis=1, keepdims=True)
        result = r.att[which] * factor + jnp.dot(
            weight.astype(bf16), value, preferred_element_type=f32
        )
        r.answer[which] = (result / total).reshape(8, 8, head)
        for g in range(8):
            value = r.answer[which, :, g, :]
            at = pl.ds((which * 8 + g) * head, head)
            for s in range(4):
                att_out[s, :, at] = value[2 * s : 2 * s + 2].astype(bf16)

    steps = dict(
        F=forward,
        X=spread_x,
        Y=spread_z,
        A=cached,
        B=stage0,
        C=own,
        D=stage1,
        E=stage2,
        G=stage3,
        H=stage4,
        I=z_stage2,
        J=z_stage3,
        K=z_stage4,
        L=z_stage5,
        P=new0,
        Q=new1,
        R=new2,
        S=new3,
    )
    order = [(word[0], int(word[1])) for word in ORDER]
    turn(other)
    def settle():
        for unit in range(UNITS):
            if PLACES[unit][0] == 0:
                pl.when(x != y)(lambda: t_copy(unit).wait_send())
            else:
                t_copy(unit).wait_send()
        for index in range(6):
            cot_copy(index).wait_send()
        for which in range(2):
            for s in range(4):
                store_copy(which, s).wait()

    for i, (name, place) in enumerate(order):
        if i == len(order) - 2:
            settle()
        steps[name](place)
        if (name, place) == ('A', 3):
            spread_done()


def last(gradient, master, first, second, new_kv, attended, *results):
    values = (*adam(gradient[...], master[...], first[...], second[...]), new_kv[...], attended[...])
    for result, value in zip(results, values):
        result[...] = value


def shards(
    features,
    kv_cotangent,
    master_weight,
    first_moment,
    second_moment,
    decode_inputs,
    queries,
    kv_cache,
    cache_lengths,
):
    tokens = features.shape[0]
    rows, columns = master_weight.shape
    steps, own_rows, width = decode_inputs.shape
    heads, slots, head = kv_cache.shape[2:]
    shapes = scratch(rows, columns, tokens, slots, head)
    in_vmem = pl.BlockSpec(memory_space=pltpu.VMEM)
    anywhere = pl.BlockSpec(memory_space=pl.ANY)
    gradient, new_kv, attended = pl.pallas_call(
        functools.partial(kernel, tuple(shapes)),
        out_shape=(
            jax.ShapeDtypeStruct((rows, columns), f32),
            jax.ShapeDtypeStruct((steps, own_rows, columns), bf16),
            jax.ShapeDtypeStruct(queries.shape, bf16),
        ),
        in_specs=[pl.BlockSpec(memory_space=pltpu.SMEM)] + [anywhere] * 8,
        out_specs=(anywhere, in_vmem, in_vmem),
        scratch_shapes=list(shapes.values()),
        compiler_params=pltpu.CompilerParams(
            collective_id=0, has_side_effects=True, vmem_limit_bytes=56 * 2**20
        ),
        name="fused_step",
    )(
        cache_lengths,
        queries,
        decode_inputs,
        features,
        kv_cotangent,
        master_weight,
        first_moment,
        second_moment,
        kv_cache,
    )
    like = jax.ShapeDtypeStruct((rows, columns), f32)
    return pl.pallas_call(
        last,
        out_shape=(
            like,
            like,
            like,
            jax.ShapeDtypeStruct(new_kv.shape, bf16),
            jax.ShapeDtypeStruct(attended.shape, bf16),
        ),
        in_specs=[in_vmem] * 6,
        out_specs=[in_vmem] * 5,
        name="last",
    )(gradient, master_weight, first_moment, second_moment, new_kv, attended)


def solution(mesh):
    in_specs = (
        P(("learn", "dp"), "tp"),
        P(("learn", "dp"), "tp"),
        P(("learn", "dp"), "tp"),
        P(("learn", "dp"), "tp"),
        P(("learn", "dp"), "tp"),
        P(None, ("learn", "dp"), None),
        P(None, ("learn", "dp"), "tp"),
        P(None, ("learn", "dp"), "tp", None, None),
        P(("learn", "dp")),
    )
    out_specs = (
        P(("learn", "dp"), "tp"),
        P(("learn", "dp"), "tp"),
        P(("learn", "dp"), "tp"),
        P(None, ("learn", "dp"), "tp"),
        P(None, ("learn", "dp"), "tp"),
    )
    return jax.shard_map(shards, mesh=mesh, in_specs=in_specs, out_specs=out_specs, check_vma=False)
```
